256 devices in a mesh: node: 16 (over x, y), feat: 16 (over z, core).
Axes of the slice: x: 4, y: 4, z: 8, core: 2. Of those that a mesh axis runs over, the one named last changes fastest.
Arguments:
- feats_t: float32 [512, 16384], P('feat', 'node'), may hold values from -6 to 6
- weight: float32 [512, 512], P(None, 'feat'), may hold values from -0.25 to 0.25
- cot_t: float32 [512, 16384], P('feat', 'node'), may hold values from -6 to 6
- tiles: float32 [128, 8, 128, 128], P('node'), may hold values from -0.1875 to 0.1875
- col_ids: int32 [128, 8], P('node'), may hold values from 0 to 127, as said below
- counts: int32 [128], P('node'), may hold values from 1 to 8, as said below
Outputs:
- out_t: float32 [512, 16384], P('feat', 'node')
- grad_feats: float32 [512, 16384], P('feat', 'node')
- grad_weight: float32 [512, 512], P(None, 'feat')
The draws below stay inside these ranges and needn't reach their ends.
Inputs may be any that keep to these rules, and one draw needn't show every extreme that they name: `col_ids`: column block c belongs to node index c // 8. Among the 64 slots of one node index's row blocks, at most 4 name column blocks of any one node index, and some node index is named by exactly 4; ids may repeat within a row block. `counts`: row block 0 has all 8 slots live; loads differ between devices.
All inputs are finite; a program needn't handle non-finite values.
Results may differ from the reference program's by a relative error of at most 0.0001.
Values sent between devices are 32-bit elements; how exact they have to be, the bound alone decides.
A program may use at most 64 MiB of HBM per device.

```python
import jax
import jax.numpy as jnp
from jax import lax

F = 512
NB_DEV = 8
K = 8
NBLK = 128
NODES = 16384


def draw_col_ids(key, part):
    key = jax.random.fold_in(key, 2)
    perm_key, rot_key, within_key = jax.random.split(key, 3)
    owners_all = NBLK // NB_DEV
    slot_total = NB_DEV * K
    perm_keys = jax.random.split(perm_key, owners_all)
    places = jax.vmap(lambda k: jax.random.permutation(k, slot_total))(perm_keys)
    rotation = jax.random.randint(rot_key, (owners_all, 1), 0, owners_all)
    owner = (places + rotation) % owners_all
    within = jax.random.randint(within_key, (owners_all, slot_total), 0, NB_DEV)
    ids = owner * NB_DEV + within
    return ids.reshape(NBLK, K).astype(jnp.int32)


def draw_counts(key, part):
    key = jax.random.fold_in(key, 1)
    level_key, count_key = jax.random.split(key)
    levels = jax.random.randint(level_key, (NBLK // NB_DEV,), 0, 4)
    block_levels = jnp.repeat(levels, NB_DEV)
    upper = 2 + (block_levels + 1) * K // 2
    drawn = jax.random.randint(count_key, (NBLK,), 1, upper)
    drawn = jnp.minimum(drawn, K)
    return drawn.at[0].set(K).astype(jnp.int32)


def steps_of(own_key, dims, shards, smallest, high):
    def one(position, parts):
        draws = jax.random.uniform(jax.random.fold_in(jax.random.fold_in(own_key, 6), position), (parts,), jnp.float32, smallest / len(shards), high / len(shards))
        return jnp.repeat(jnp.exp(draws), dims[position] // parts).reshape((-1,) + (1,) * (len(dims) - position - 1))

    gain = one(*shards[0])
    for cut in shards[1:]:
        gain = gain * one(*cut)
    return gain


def scatter_about(key, dims, scale, most, pieces=(), held_as=jnp.bfloat16):
    loudness = steps_of(key, dims, pieces, -0.22, 0.18) if pieces else 1.0
    values = jax.random.normal(key, dims, jnp.float32) * scale * loudness
    return jnp.minimum(jnp.maximum(values, -most), most).astype(held_as)


def setup_inputs(seed: int = 0) -> dict:
    key_of = jax.random.split(jax.random.key(seed), 7)
    return {
        "feats_t": scatter_about(key_of[0], (F, NODES), 1.0, 6.0, ((0, 16), (1, 16)), jnp.float32),
        "weight": scatter_about(key_of[1], (F, F), F ** -0.5, 0.25, ((1, 16),), jnp.float32),
        "cot_t": scatter_about(key_of[2], (F, NODES), 1.0, 6.0, ((0, 16), (1, 16)), jnp.float32),
        "tiles": scatter_about(key_of[3], (NBLK, K, 128, 128), (128 * K) ** -0.5, 0.1875, ((0, 16),), jnp.float32),
        "col_ids": draw_col_ids(jax.random.fold_in(key_of[6], 71), 0),
        "counts": draw_counts(jax.random.fold_in(key_of[6], 71), 0),
    }


HIGH = lax.Precision.HIGHEST


def reference(feats_t, weight, cot_t, tiles, col_ids, counts):
    width = feats_t.shape[0]
    total = tiles.shape[0]
    slots = tiles.shape[1]
    blocks = feats_t.reshape(width, total, 128)
    live = (jnp.arange(slots)[None, :] < counts[:, None]).astype(jnp.float32)

    def forward_block(index):
        picked = jnp.take(blocks, col_ids[index], axis=1) * live[index][None, :, None]
        return jnp.einsum("fkc,krc->fr", picked, tiles[index], precision=HIGH)

    mixed = lax.map(forward_block, jnp.arange(total))
    mixed_t = jnp.transpose(mixed, (1, 0, 2)).reshape(width, total * 128)
    pre_t = jnp.dot(weight.T, mixed_t, precision=HIGH)
    sig = jax.nn.sigmoid(pre_t)
    out_t = pre_t * sig
    grad_pre = cot_t * (sig * (1.0 + pre_t * (1.0 - sig)))
    grad_weight = jnp.dot(mixed_t, grad_pre.T, precision=HIGH)
    grad_mixed = jnp.dot(weight, grad_pre, precision=HIGH).reshape(width, total, 128)

    def backward_block(carry, index):
        contrib = jnp.einsum("fr,krc->fkc", grad_mixed[:, index], tiles[index], precision=HIGH)
        contrib = contrib * live[index][None, :, None]
        return carry.at[:, col_ids[index]].add(contrib), None

    start_grad = jnp.zeros((width, total, 128), jnp.float32)
    grad_blocks, _ = lax.scan(backward_block, start_grad, jnp.arange(total))
    grad_feats = grad_blocks.reshape(width, total * 128)
    return out_t, grad_feats, grad_weight
```

```python
import jax
import jax.numpy as jnp
from jax import lax
from jax.experimental import pallas as pl
from jax.experimental.pallas import tpu as pltpu
from jax.sharding import PartitionSpec as P

MESH = pl.DeviceIdType.MESH
F32 = jnp.float32
BF16 = jnp.bfloat16
I32 = jnp.int32
NN = (((1,), (0,)), ((), ()))
NT = (((1,), (1,)), ((), ()))
FAR = (4, 3, 5, 2, 6, 1, 7)


def split(v):
    hi = v.astype(BF16)
    return hi, (v - hi.astype(F32)).astype(BF16)


def mm(a, b, dims):
    return lax.dot_general(a, b, dims, preferred_element_type=F32)


def kernel(
    feats, wt, cot, tiles, cols_h, counts_h,
    out, gf, gwt,
    t32, tb, f3, av0, av1, sv, rv, mx, mv, wa, wst, wn, ca,
    oo, orv, pv, px, gs, gv, gwp, gwr, gw0, gwa, gw1, gwb,
    cv, sb, qv, dv, ev, tab, tabr, tabs, tabrs, cols, counts,
    sem_t, sem_s, sem_i,
    s1, r1, s1t, r1t, s2, r2, sw, rw, sc, rc, sm, rm, sf, rf, sp, rp,
    so, ro, sg, rg, sgw, rgw, sq, rq, se, re, sga, rga, sgb, rgb,
):
    node = lax.axis_index("node")
    feat = lax.axis_index("feat")
    x, y = lax.div(node, 4), lax.rem(node, 4)
    z, c = lax.div(feat, 2), lax.rem(feat, 2)
    oc = 1 - c

    def at_x(d):
        return lax.rem(x + d, 4)

    def at_y(d):
        return lax.rem(y + d, 4)

    def at_z(d):
        return lax.rem(z + d, 8)

    def xdev(d):
        return (at_x(d) * 4 + y, feat)

    def ydev(d):
        return (x * 4 + at_y(d), feat)

    def zdev(d):
        return (node, at_z(d) * 2 + c)

    cdev = (node, z * 2 + oc)
    pending = []

    def send(src, dst, device, ss, rs):
        cp = pltpu.make_async_remote_copy(
            src_ref=src, dst_ref=dst, send_sem=ss, recv_sem=rs,
            device_id=device, device_id_type=MESH,
        )
        cp.start()
        pending.append(cp)
        return cp

    ids = [
        pltpu.make_async_copy(cols_h, cols, sem_i.at[0]),
        pltpu.make_async_copy(counts_h, counts, sem_i.at[1]),
    ]
    fcopies = [
        pltpu.make_async_copy(feats.at[:, pl.ds(128 * w, 128)], f3.at[w], sem_i.at[2 + w])
        for w in range(8)
    ]
    own = [
        pltpu.make_async_copy(wt, wa.at[z], sem_i.at[10]),
        pltpu.make_async_copy(cot.at[:, pl.ds(pl.multiple_of(z * 128, 128), 128)], ca.at[z], sem_i.at[11]),
    ]
    for cp in ids + fcopies + own:
        cp.start()
    for b in range(8):
        pltpu.make_async_copy(tiles.at[b], t32.at[b], sem_t.at[b]).start()
    barrier = pltpu.get_barrier_semaphore()
    peers = [xdev(d) for d in (1, 2, 3)] + [ydev(d) for d in (1, 2, 3)]
    peers += [zdev(d) for d in range(1, 8)] + [cdev]
    for p in peers:
        pl.semaphore_signal(barrier, 1, device_id=p, device_id_type=MESH)

    for cp in ids:
        cp.wait()
    lane8 = lax.broadcasted_iota(I32, (8, 128), 1)
    sub8 = lax.broadcasted_iota(I32, (8, 128), 0)
    by_lane = jnp.full((8, 128), 1024, I32)
    for s in range(64):
        by_lane = jnp.where(lane8 == s, cols[s // 8, s % 8], by_lane)
    place_l = jnp.zeros((8, 128), I32)
    rows = []
    for g in range(8):
        by_sub = jnp.zeros((8, 128), I32)
        for k in range(8):
            by_sub = jnp.where(sub8 == k, cols[g, k], by_sub)
        rows.append(by_sub)
    own_l = lax.shift_right_logical(by_lane, 3)
    slot_sum = jnp.zeros((8, 128), I32)
    want_sum = jnp.zeros((8, 128), I32)
    for g in range(8):
        own_s = lax.shift_right_logical(rows[g], 3)
        slot_s = sub8 + 8 * g
        same = own_s == own_l
        place_l = place_l + jnp.where(same & (slot_s < lane8), 1, 0)
        rank = jnp.sum(jnp.where(same & (lane8 < slot_s), 1, 0), axis=1, keepdims=True)
        hit = (own_s * 4 + rank) == lane8
        slot_sum = slot_sum + jnp.where(hit, slot_s, 0)
        want_sum = want_sum + jnp.where(hit, rows[g] & 7, 0)
    place = own_l * 4 + jnp.sum(place_l, axis=0, keepdims=True)
    slot_of = jnp.sum(slot_sum, axis=0, keepdims=True)
    want = jnp.sum(want_sum, axis=0, keepdims=True)
    table = jnp.where(sub8 == 0, place, jnp.where(sub8 == 1, slot_of, want))
    tab[...] = table
    tabr[0, y] = table
    tabr[1, x] = table

    for cp in fcopies:
        cp.wait()
    av0[x] = f3[:, 0:16]
    av1[y] = f3[:, 16:32]
    pl.semaphore_wait(barrier, len(peers))

    tx = [send(tab, tabr.at[1, x], xdev(d), s1t.at[0, d], r1t.at[0, d]) for d in (1, 2, 3)]
    ty = [send(tab, tabr.at[0, y], ydev(d), s1t.at[1, d], r1t.at[1, d]) for d in (1, 2, 3)]
    fx = [send(f3.at[:, pl.ds(0, 16)], av0.at[x], xdev(d), s1.at[0, d], r1.at[0, d]) for d in (2, 1, 3)]
    fy = [send(f3.at[:, pl.ds(16, 16)], av1.at[y], ydev(d), s1.at[1, d], r1.at[1, d]) for d in (2, 1, 3)]
    cz = [send(cot.at[:, pl.ds(pl.multiple_of(at_z(d) * 128, 128), 128)], ca.at[z], zdev(d), sc.at[d], rc.at[d]) for d in FAR]
    wz = [send(wt, wa.at[z], zdev(d), sw.at[d], rw.at[d]) for d in FAR]
    to_s = pltpu.make_async_copy(tab, tabs, sem_s.at[0])
    to_s.start()

    def convert(b, carry):
        pltpu.make_async_copy(tiles.at[b], t32.at[b], sem_t.at[b]).wait()
        for k in range(8):
            live = jnp.where(k < counts[b], 1.0, 0.0).astype(F32)
            hi, lo = split(t32[b, k] * live)
            q = 128 * (k % 2)
            tb[b, k // 2, 0:128, q : q + 128] = hi
            tb[b, k // 2, 128:256, q : q + 128] = lo
        return carry

    lax.fori_loop(0, 8, convert, 0)

    to_s.wait()
    for cp in tx + ty:
        cp.wait_recv()
    to_rs = pltpu.make_async_copy(tabr, tabrs, sem_s.at[1])
    to_rs.start()
    to_rs.wait()

    for cp in fx:
        cp.wait_recv()
    leg2 = []
    for d in (2, 1, 3, 0):
        yd = at_y(d)
        for xo in range(4):
            for r in range(4):
                w = tabrs[0, yd, 2, (xo * 4 + y) * 4 + r]
                block = av0[xo, w]
                if d:
                    sv[0, d, xo, r] = block
                else:
                    rv[xo, y, r, 0:16] = block
        if d:
            leg2.append(
                send(sv.at[0, d], rv.at[:, y, :, pl.ds(0, 16)], ydev(d), s2.at[0, d], r2.at[0, d])
            )
    for cp in fy:
        cp.wait_recv()
    for d in (2, 1, 3, 0):
        xd = at_x(d)
        for yo in range(4):
            for r in range(4):
                w = tabrs[1, xd, 2, (x * 4 + yo) * 4 + r]
                block = av1[yo, w]
                if d:
                    sv[1, d, yo, r] = block
                else:
                    rv[x, yo, r, 16:32] = block
        if d:
            leg2.append(
                send(sv.at[1, d], rv.at[x, :, :, pl.ds(16, 16)], xdev(d), s2.at[1, d], r2.at[1, d])
            )

    for cp in wz:
        cp.wait_recv()
    for cp in own:
        cp.wait()
    for q in range(8):
        hi, lo = split(wa[q])
        wst[32 * q : 32 * q + 32] = hi
        wst[256 + 32 * q : 288 + 32 * q] = lo
    for g in range(4):
        turned = jnp.transpose(wa[:, :, 128 * g : 128 * g + 128].reshape(256, 128))
        hi, lo = split(turned)
        wn[128 * g : 128 * g + 128] = hi
        wn[512 + 128 * g : 640 + 128 * g] = lo

    for cp in leg2:
        cp.wait_recv()

    mz = []
    for d in FAR + (0,):
        b = at_z(d)
        acc = None
        for kp in range(4):
            parts = []
            for k in (2 * kp, 2 * kp + 1):
                p = tabs[0, b * 8 + k]
                parts.append(
                    split(rv[lax.shift_right_logical(p, 4), lax.shift_right_logical(p, 2) & 3, p & 3])
                )
            lhs = jnp.concatenate(
                [
                    jnp.concatenate([parts[0][0], parts[1][0]], axis=1),
                    jnp.concatenate([parts[0][1], parts[1][1]], axis=1),
                ],
                axis=0,
            )
            term = mm(lhs, tb[b, kp], NT)
            acc = term if acc is None else acc + term
        mixed = (acc[32:64, 128:256] + acc[32:64, 0:128] + acc[0:32, 128:256]) + acc[0:32, 0:128]
        if d:
            mx[d] = mixed
            mz.append(send(mx.at[d], mv.at[z, c], zdev(d), sm.at[d], rm.at[d]))
        else:
            mv[z, c] = mixed
    fz = [send(mv.at[z, c], mv.at[z, c], cdev, sf.at[0], rf.at[0])]
    for i, d in enumerate(FAR):
        mz[i].wait_recv()
        q = at_z(8 - d)
        fz.append(send(mv.at[q, c], mv.at[q, c], cdev, sf.at[d], rf.at[d]))
    for cp in cz:
        cp.wait_recv()
    for cp in fz:
        cp.wait_recv()

    hi, lo = split(mv[...].reshape(512, 128))
    mhl = jnp.concatenate([hi, lo], axis=1)
    r = mm(wst[...], mhl, NN)
    pre = (r[256:512, 128:256] + r[256:512, 0:128] + r[0:256, 128:256]) + r[0:256, 0:128]
    sig = jax.nn.sigmoid(pre)
    gp = ca[...].reshape(256, 128) * (sig * (1.0 + pre * (1.0 - sig)))
    ghi, glo = split(gp)
    r = mm(wn[...], jnp.concatenate([ghi, glo], axis=1), NN)
    part = (r[512:1024, 128:256] + r[512:1024, 0:128] + r[0:512, 128:256]) + r[0:512, 0:128]
    pv[...] = part.reshape(8, 2, 32, 128)
    xc = send(pv.at[:, oc], px, cdev, sp, rp)
    oo[...] = (pre * sig).reshape(8, 32, 128)
    g2 = jnp.concatenate(
        [jnp.concatenate([ghi, ghi], axis=1), jnp.concatenate([glo, glo], axis=1)], axis=0
    )
    r = mm(g2, mhl, NT)
    gwp[...] = (r[0:256] + r[256:512]).reshape(8, 32, 512)
    xc.wait_recv()
    gz = []
    gs[...] = pv[:, c] + px[...]
    for d in FAR:
        gz.append(send(gs.at[at_z(d)], gv.at[z], zdev(d), sg.at[d], rg.at[d]))
    gv[z] = gs[z]
    oz = [send(oo.at[at_z(d)], orv.at[z], zdev(d), so.at[d], ro.at[d]) for d in FAR]
    wz2 = [send(gwp.at[at_z(d)], gwr.at[z], zdev(d), sgw.at[d], rgw.at[d]) for d in FAR]
    orv[z] = oo[z]
    gwr[z] = gwp[z]

    arrivals = {d: cp for d, cp in zip(FAR, gz)}
    for d in (0, 1, 7, 2, 6, 3, 5, 4):
        if d:
            arrivals[d].wait_recv()
        b = at_z(8 - d)
        ghi, glo = split(gv[b])
        lhs = jnp.concatenate(
            [jnp.concatenate([ghi, ghi], axis=1), jnp.concatenate([glo, glo], axis=1)], axis=0
        )
        for kp in range(4):
            r = mm(lhs, tb[b, kp], NN)
            r = r[0:32] + r[32:64]
            cv[b * 8 + 2 * kp] = r[:, 0:128]
            cv[b * 8 + 2 * kp + 1] = r[:, 128:256]

    q0, q1 = [], []
    for d in (2, 1, 3, 0):
        yd = at_y(d)
        for xo in range(4):
            for r in range(4):
                s = tabs[1, (xo * 4 + yd) * 4 + r]
                piece = cv[s, 0:16]
                if d:
                    sb[0, d, xo, r] = piece
                else:
                    qv[0, y, xo, r] = piece
        if d:
            q0.append(send(sb.at[0, d], qv.at[0, y], ydev(d), sq.at[0, d], rq.at[0, d]))
    for d in (2, 1, 3, 0):
        xd = at_x(d)
        for yo in range(4):
            for r in range(4):
                s = tabs[1, (xd * 4 + yo) * 4 + r]
                piece = cv[s, 16:32]
                if d:
                    sb[1, d, yo, r] = piece
                else:
                    qv[1, x, yo, r] = piece
        if d:
            q1.append(send(sb.at[1, d], qv.at[1, x], xdev(d), sq.at[1, d], rq.at[1, d]))

    for cp in q0:
        cp.wait_recv()
    e0, e1 = [], []
    for d in (2, 1, 3, 0):
        xd = at_x(d)
        total = [jnp.zeros((16, 128), F32) for _ in range(8)]
        for src in range(4):
            for r in range(4):
                w = tabrs[0, src, 2, (xd * 4 + y) * 4 + r]
                piece = qv[0, src, xd, r]
                for i in range(8):
                    total[i] = total[i] + jnp.where(w == i, 1.0, 0.0).astype(F32) * piece
        for i in range(8):
            if d:
                dv[0, d, i] = total[i]
            else:
                ev[0, x, i] = total[i]
        if d:
            e0.append(send(dv.at[0, d], ev.at[0, x], xdev(d), se.at[0, d], re.at[0, d]))
    for cp in q1:
        cp.wait_recv()
    for d in (2, 1, 3, 0):
        yd = at_y(d)
        total = [jnp.zeros((16, 128), F32) for _ in range(8)]
        for src in range(4):
            for r in range(4):
                w = tabrs[1, src, 2, (x * 4 + yd) * 4 + r]
                piece = qv[1, src, yd, r]
                for i in range(8):
                    total[i] = total[i] + jnp.where(w == i, 1.0, 0.0).astype(F32) * piece
        for i in range(8):
            if d:
                dv[1, d, i] = total[i]
            else:
                ev[1, y, i] = total[i]
        if d:
            e1.append(send(dv.at[1, d], ev.at[1, y], ydev(d), se.at[1, d], re.at[1, d]))

    for cp in wz2:
        cp.wait_recv()
    total = gwr[0]
    for q in range(1, 8):
        total = total + gwr[q]
    gw0[0] = total[0:16]
    gw0[1] = total[16:32]
    ga = [send(gw0.at[0], gwa.at[0, x], xdev(d), sga.at[0, d], rga.at[0, d]) for d in (2, 1, 3)]
    ga += [send(gw0.at[1], gwa.at[1, y], ydev(d), sga.at[1, d], rga.at[1, d]) for d in (2, 1, 3)]
    gwa[0, x] = total[0:16]
    gwa[1, y] = total[16:32]
    for cp in oz:
        cp.wait_recv()
    for b in range(8):
        out[:, 128 * b : 128 * b + 128] = orv[b]
    for cp in ga:
        cp.wait_recv()
    for h in range(2):
        half = (gwa[h, 0] + gwa[h, 1]) + (gwa[h, 2] + gwa[h, 3])
        gw1[h] = half
    gb = [send(gw1.at[0], gwb.at[0, y], ydev(d), sgb.at[0, d], rgb.at[0, d]) for d in (2, 1, 3)]
    gb += [send(gw1.at[1], gwb.at[1, x], xdev(d), sgb.at[1, d], rgb.at[1, d]) for d in (2, 1, 3)]
    gwb[0, y] = gw1[0]
    gwb[1, x] = gw1[1]
    for cp in e0 + e1:
        cp.wait_recv()
    for h in range(2):
        for w in range(8):
            gf[16 * h : 16 * h + 16, 128 * w : 128 * w + 128] = (ev[h, 0, w] + ev[h, 1, w]) + (
                ev[h, 2, w] + ev[h, 3, w]
            )
    for cp in gb:
        cp.wait_recv()
    for h in range(2):
        gwt[16 * h : 16 * h + 16] = (gwb[h, 0] + gwb[h, 1]) + (gwb[h, 2] + gwb[h, 3])
    for cp in pending:
        cp.wait_send()


def on_device(feats_t, weight, cot_t, tiles, col_ids, counts):
    vmem = pl.BlockSpec(memory_space=pltpu.VMEM)
    hbm = pl.BlockSpec(memory_space=pltpu.HBM)

    def v(*shape):
        return pltpu.VMEM(shape, F32)

    def dma(*shape):
        return pltpu.SemaphoreType.DMA(shape)

    scratch = [
        v(8, 8, 128, 128),
        pltpu.VMEM((8, 4, 256, 256), BF16),
        v(8, 32, 128),
        v(4, 8, 16, 128),
        v(4, 8, 16, 128),
        v(2, 4, 4, 4, 16, 128),
        v(4, 4, 4, 32, 128),
        v(8, 32, 128),
        v(8, 2, 32, 128),
        v(8, 32, 512),
        pltpu.VMEM((512, 512), BF16),
        pltpu.VMEM((1024, 256), BF16),
        v(8, 32, 128),
        v(8, 32, 128),
        v(8, 32, 128),
        v(8, 2, 32, 128),
        v(8, 32, 128),
        v(8, 32, 128),
        v(8, 32, 128),
        v(8, 32, 512),
        v(8, 32, 512),
        v(2, 16, 512),
        v(2, 4, 16, 512),
        v(2, 16, 512),
        v(2, 4, 16, 512),
        v(64, 32, 128),
        v(2, 4, 4, 4, 16, 128),
        v(2, 4, 4, 4, 16, 128),
        v(2, 4, 8, 16, 128),
        v(2, 4, 8, 16, 128),
        pltpu.VMEM((8, 128), I32),
        pltpu.VMEM((2, 4, 8, 128), I32),
        pltpu.SMEM((8, 128), I32),
        pltpu.SMEM((2, 4, 8, 128), I32),
        pltpu.SMEM((8, 8), I32),
        pltpu.SMEM((8,), I32),
        dma(8), dma(2), dma(12),
        dma(2, 4), dma(2, 4), dma(2, 4), dma(2, 4), dma(2, 4), dma(2, 4),
        dma(8), dma(8), dma(8), dma(8), dma(8), dma(8), dma(8), dma(8),
        pltpu.SemaphoreType.DMA, pltpu.SemaphoreType.DMA,
        dma(8), dma(8), dma(8), dma(8), dma(8), dma(8),
        dma(2, 4), dma(2, 4), dma(2, 4), dma(2, 4),
        dma(2, 4), dma(2, 4), dma(2, 4), dma(2, 4),
    ]
    out, gf, gwt = pl.pallas_call(
        kernel,
        out_shape=(
            jax.ShapeDtypeStruct((32, 1024), F32),
            jax.ShapeDtypeStruct((32, 1024), F32),
            jax.ShapeDtypeStruct((32, 512), F32),
        ),
        in_specs=[hbm] * 6,
        out_specs=(vmem, vmem, vmem),
        scratch_shapes=scratch,
        name="graph_layer",
        cost_estimate=pl.CostEstimate(flops=10**9, bytes_accessed=6 * 10**6, transcendentals=32768),
        compiler_params=pltpu.CompilerParams(
            collective_id=0, has_side_effects=True, vmem_limit_bytes=61936 * 1024
        ),
    )(feats_t, weight.T, cot_t, tiles, col_ids, counts)
    return out, gf, gwt.T


def solution(mesh):
    return jax.shard_map(
        on_device,
        mesh=mesh,
        in_specs=(
            P("feat", "node"),
            P(None, "feat"),
            P("feat", "node"),
            P("node", None, None, None),
            P("node", None),
            P("node"),
        ),
        out_specs=(P("feat", "node"), P("feat", "node"), P(None, "feat")),
        check_vma=False,
    )
```

```python
import jax
import jax.numpy as jnp
from jax import lax
from jax.experimental import pallas as pl
from jax.experimental.pallas import tpu as pltpu
from jax.sharding import PartitionSpec as P

MESH = pl.DeviceIdType.MESH
F32 = jnp.float32
BF16 = jnp.bfloat16
I32 = jnp.int32
NN = (((1,), (0,)), ((), ()))
NT = (((1,), (1,)), ((), ()))
FAR = (4, 3, 5, 2, 6, 1, 7)


def split(v):
    hi = v.astype(BF16)
    return hi, (v - hi.astype(F32)).astype(BF16)


def mm(a, b, dims):
    return lax.dot_general(a, b, dims, preferred_element_type=F32)


def kernel(
    feats, wt, cot, tiles, cols_h, counts_h,
    out, gf, gwt,
    t32, tb, f3, av0, av1, sv, rv, mx, mv, wa, wst, wn, ca,
    oo, orv, pv, px, gs, gv, wp0, wp1, ga0, ga1, gbs, gbr, gcs, gcr, ger,
    cv, sb, qv, dv, ev, tab, tabr, tabs, tabrs, cols, counts,
    sem_t, sem_s, sem_i,
    s1, r1, s1t, r1t, s2, r2, sw, rw, sc, rc, sm, rm, sf, rf, sp, rp,
    so, ro, sg, rg, sgw, rgw, sq, rq, se, re, sga, rga, sgb, rgb, sge, rge,
):
    node = lax.axis_index("node")
    feat = lax.axis_index("feat")
    x, y = lax.div(node, 4), lax.rem(node, 4)
    z, c = lax.div(feat, 2), lax.rem(feat, 2)
    oc = 1 - c

    def at_x(d):
        return lax.rem(x + d, 4)

    def at_y(d):
        return lax.rem(y + d, 4)

    def at_z(d):
        return lax.rem(z + d, 8)

    def xdev(d):
        return (at_x(d) * 4 + y, feat)

    def ydev(d):
        return (x * 4 + at_y(d), feat)

    def zdev(d):
        return (node, at_z(d) * 2 + c)

    cdev = (node, z * 2 + oc)
    pending = []

    def send(src, dst, device, ss, rs):
        cp = pltpu.make_async_remote_copy(
            src_ref=src, dst_ref=dst, send_sem=ss, recv_sem=rs,
            device_id=device, device_id_type=MESH,
        )
        cp.start()
        pending.append(cp)
        return cp

    ids = [
        pltpu.make_async_copy(cols_h, cols, sem_i.at[0]),
        pltpu.make_async_copy(counts_h, counts, sem_i.at[1]),
    ]
    fcopies = [
        pltpu.make_async_copy(feats.at[:, pl.ds(128 * w, 128)], f3.at[w], sem_i.at[2 + w])
        for w in range(8)
    ]
    own = [
        pltpu.make_async_copy(wt, wa.at[z], sem_i.at[10]),
        pltpu.make_async_copy(cot.at[:, pl.ds(pl.multiple_of(z * 128, 128), 128)], ca.at[z], sem_i.at[11]),
    ]
    for cp in ids + fcopies + own:
        cp.start()
    for b in range(8):
        pltpu.make_async_copy(tiles.at[b], t32.at[b], sem_t.at[b]).start()
    barrier = pltpu.get_barrier_semaphore()
    peers = [xdev(d) for d in (1, 2, 3)] + [ydev(d) for d in (1, 2, 3)]
    peers += [zdev(d) for d in range(1, 8)] + [cdev]
    for p in peers:
        pl.semaphore_signal(barrier, 1, device_id=p, device_id_type=MESH)

    for cp in fcopies:
        cp.wait()
    av0[x] = f3[:, 0:16]
    av1[y] = f3[:, 16:32]
    pl.semaphore_wait(barrier, len(peers))

    fx = [send(f3.at[:, pl.ds(0, 16)], av0.at[x], xdev(d), s1.at[0, d], r1.at[0, d]) for d in (2, 1, 3)]
    fy = [send(f3.at[:, pl.ds(16, 16)], av1.at[y], ydev(d), s1.at[1, d], r1.at[1, d]) for d in (2, 1, 3)]
    cz = [send(cot.at[:, pl.ds(pl.multiple_of(at_z(d) * 128, 128), 128)], ca.at[z], zdev(d), sc.at[d], rc.at[d]) for d in FAR]
    wz = [send(wt, wa.at[z], zdev(d), sw.at[d], rw.at[d]) for d in FAR]

    for cp in ids:
        cp.wait()
    lane8 = lax.broadcasted_iota(I32, (8, 128), 1)
    sub8 = lax.broadcasted_iota(I32, (8, 128), 0)
    by_lane = jnp.full((8, 128), 1024, I32)
    for s in range(64):
        by_lane = jnp.where(lane8 == s, cols[s // 8, s % 8], by_lane)
    place_l = jnp.zeros((8, 128), I32)
    rows = []
    for g in range(8):
        by_sub = jnp.zeros((8, 128), I32)
        for k in range(8):
            by_sub = jnp.where(sub8 == k, cols[g, k], by_sub)
        rows.append(by_sub)
    own_l = lax.shift_right_logical(by_lane, 3)
    slot_sum = jnp.zeros((8, 128), I32)
    want_sum = jnp.zeros((8, 128), I32)
    for g in range(8):
        own_s = lax.shift_right_logical(rows[g], 3)
        slot_s = sub8 + 8 * g
        same = own_s == own_l
        place_l = place_l + jnp.where(same & (slot_s < lane8), 1, 0)
        rank = jnp.sum(jnp.where(same & (lane8 < slot_s), 1, 0), axis=1, keepdims=True)
        hit = (own_s * 4 + rank) == lane8
        slot_sum = slot_sum + jnp.where(hit, slot_s, 0)
        want_sum = want_sum + jnp.where(hit, rows[g] & 7, 0)
    place = own_l * 4 + jnp.sum(place_l, axis=0, keepdims=True)
    slot_of = jnp.sum(slot_sum, axis=0, keepdims=True)
    want = jnp.sum(want_sum, axis=0, keepdims=True)
    table = jnp.where(sub8 == 0, place, jnp.where(sub8 == 1, slot_of, want))
    tab[...] = table
    tabr[0, y] = table
    tabr[1, x] = table

    tx = [send(tab, tabr.at[1, x], xdev(d), s1t.at[0, d], r1t.at[0, d]) for d in (1, 2, 3)]
    ty = [send(tab, tabr.at[0, y], ydev(d), s1t.at[1, d], r1t.at[1, d]) for d in (1, 2, 3)]
    to_s = pltpu.make_async_copy(tab, tabs, sem_s.at[0])
    to_s.start()

    to_s.wait()
    for cp in tx + ty:
        cp.wait_recv()
    to_rs = pltpu.make_async_copy(tabr, tabrs, sem_s.at[1])
    to_rs.start()
    to_rs.wait()

    for cp in fx:
        cp.wait_recv()
    leg2 = []
    for d in (2, 1, 3, 0):
        yd = at_y(d)
        for xo in range(4):
            for r in range(4):
                w = tabrs[0, yd, 2, (xo * 4 + y) * 4 + r]
                block = av0[xo, w]
                if d:
                    sv[0, d, xo, r] = block
                else:
                    rv[xo, y, r, 0:16] = block
        if d:
            leg2.append(
                send(sv.at[0, d], rv.at[:, y, :, pl.ds(0, 16)], ydev(d), s2.at[0, d], r2.at[0, d])
            )
    for cp in fy:
        cp.wait_recv()
    for d in (2, 1, 3, 0):
        xd = at_x(d)
        for yo in range(4):
            for r in range(4):
                w = tabrs[1, xd, 2, (x * 4 + yo) * 4 + r]
                block = av1[yo, w]
                if d:
                    sv[1, d, yo, r] = block
                else:
                    rv[x, yo, r, 16:32] = block
        if d:
            leg2.append(
                send(sv.at[1, d], rv.at[x, :, :, pl.ds(16, 16)], xdev(d), s2.at[1, d], r2.at[1, d])
            )

    def convert(b, carry):
        pltpu.make_async_copy(tiles.at[b], t32.at[b], sem_t.at[b]).wait()
        for k in range(8):
            live = jnp.where(k < counts[b], 1.0, 0.0).astype(F32)
            hi, lo = split(t32[b, k] * live)
            q = 128 * (k % 2)
            tb[b, k // 2, 0:128, q : q + 128] = hi
            tb[b, k // 2, 128:256, q : q + 128] = lo
        return carry

    lax.fori_loop(0, 8, convert, 0)

    for cp in leg2:
        cp.wait_recv()

    mz = []
    for d in FAR + (0,):
        b = at_z(d)
        acc = None
        for kp in range(4):
            parts = []
            for k in (2 * kp, 2 * kp + 1):
                p = tabs[0, b * 8 + k]
                parts.append(
                    split(rv[lax.shift_right_logical(p, 4), lax.shift_right_logical(p, 2) & 3, p & 3])
                )
            lhs = jnp.concatenate(
                [
                    jnp.concatenate([parts[0][0], parts[1][0]], axis=1),
                    jnp.concatenate([parts[0][1], parts[1][1]], axis=1),
                ],
                axis=0,
            )
            term = mm(lhs, tb[b, kp], NT)
            acc = term if acc is None else acc + term
        mixed = (acc[32:64, 128:256] + acc[32:64, 0:128] + acc[0:32, 128:256]) + acc[0:32, 0:128]
        if d:
            mx[d] = mixed
            mz.append(send(mx.at[d], mv.at[z, c], zdev(d), sm.at[d], rm.at[d]))
        else:
            mv[z, c] = mixed
    for cp in wz:
        cp.wait_recv()
    for cp in own:
        cp.wait()
    for q in range(8):
        hi, lo = split(wa[q])
        wst[32 * q : 32 * q + 32] = hi
        wst[256 + 32 * q : 288 + 32 * q] = lo
    for g in range(4):
        turned = jnp.transpose(wa[:, :, 128 * g : 128 * g + 128].reshape(256, 128))
        hi, lo = split(turned)
        wn[128 * g : 128 * g + 128] = hi
        wn[512 + 128 * g : 640 + 128 * g] = lo

    fz = [send(mv.at[z, c], mv.at[z, c], cdev, sf.at[0], rf.at[0])]
    for i, d in enumerate(FAR):
        mz[i].wait_recv()
        q = at_z(8 - d)
        fz.append(send(mv.at[q, c], mv.at[q, c], cdev, sf.at[d], rf.at[d]))
    for cp in cz:
        cp.wait_recv()
    for cp in fz:
        cp.wait_recv()

    hi, lo = split(mv[...].reshape(512, 128))
    mhl = jnp.concatenate([hi, lo], axis=1)
    r = mm(wst[...], mhl, NN)
    pre = (r[256:512, 128:256] + r[256:512, 0:128] + r[0:256, 128:256]) + r[0:256, 0:128]
    sig = jax.nn.sigmoid(pre)
    gp = ca[...].reshape(256, 128) * (sig * (1.0 + pre * (1.0 - sig)))
    ghi, glo = split(gp)
    r = mm(wn[...], jnp.concatenate([ghi, glo], axis=1), NN)
    part = (r[512:1024, 128:256] + r[512:1024, 0:128] + r[0:512, 128:256]) + r[0:512, 0:128]
    pv[...] = part.reshape(8, 2, 32, 128)
    xc = send(pv.at[:, oc], px, cdev, sp, rp)
    oo[...] = (pre * sig).reshape(8, 32, 128)
    g2 = jnp.concatenate(
        [jnp.concatenate([ghi, ghi], axis=1), jnp.concatenate([glo, glo], axis=1)], axis=0
    )
    r = mm(g2, mhl, NT)
    r = r[0:256] + r[256:512]
    for q in range(8):
        for a in range(4):
            for g in range(4):
                chunk = r[32 * q + 8 * a : 32 * q + 8 * a + 8, 128 * g : 128 * g + 128]
                if q < 4:
                    wp0[a, g, q] = chunk
                else:
                    wp1[g, a, q - 4] = chunk
    xc.wait_recv()
    gz = []
    gs[...] = pv[:, c] + px[...]
    for d in FAR:
        gz.append(send(gs.at[at_z(d)], gv.at[z], zdev(d), sg.at[d], rg.at[d]))
    gv[z] = gs[z]
    ga = [send(wp0.at[at_x(d)], ga0.at[x], xdev(d), sga.at[0, d], rga.at[0, d]) for d in (2, 1, 3)]
    ga += [send(wp1.at[at_y(d)], ga1.at[y], ydev(d), sga.at[1, d], rga.at[1, d]) for d in (2, 1, 3)]
    ga0[x] = wp0[x]
    ga1[y] = wp1[y]
    oz = [send(oo.at[at_z(d)], orv.at[z], zdev(d), so.at[d], ro.at[d]) for d in FAR]
    orv[z] = oo[z]

    arrivals = {d: cp for d, cp in zip(FAR, gz)}
    for d in (0, 1, 7, 2, 6, 3, 5, 4):
        if d:
            arrivals[d].wait_recv()
        b = at_z(8 - d)
        ghi, glo = split(gv[b])
        lhs = jnp.concatenate(
            [jnp.concatenate([ghi, ghi], axis=1), jnp.concatenate([glo, glo], axis=1)], axis=0
        )
        for kp in range(4):
            r = mm(lhs, tb[b, kp], NN)
            r = r[0:32] + r[32:64]
            cv[b * 8 + 2 * kp] = r[:, 0:128]
            cv[b * 8 + 2 * kp + 1] = r[:, 128:256]

    for cp in ga:
        cp.wait_recv()
    gbs[0] = (ga0[0] + ga0[1]) + (ga0[2] + ga0[3])
    gbs[1] = (ga1[0] + ga1[1]) + (ga1[2] + ga1[3])
    gb = [send(gbs.at[0, at_y(d)], gbr.at[0, y], ydev(d), sgb.at[0, d], rgb.at[0, d]) for d in (2, 1, 3)]
    gb += [send(gbs.at[1, at_x(d)], gbr.at[1, x], xdev(d), sgb.at[1, d], rgb.at[1, d]) for d in (2, 1, 3)]
    gbr[0, y] = gbs[0, y]
    gbr[1, x] = gbs[1, x]

    q0, q1 = [], []
    for d in (2, 1, 3, 0):
        yd = at_y(d)
        for xo in range(4):
            for r in range(4):
                s = tabs[1, (xo * 4 + yd) * 4 + r]
                piece = cv[s, 0:16]
                if d:
                    sb[0, d, xo, r] = piece
                else:
                    qv[0, y, xo, r] = piece
        if d:
            q0.append(send(sb.at[0, d], qv.at[0, y], ydev(d), sq.at[0, d], rq.at[0, d]))
    for d in (2, 1, 3, 0):
        xd = at_x(d)
        for yo in range(4):
            for r in range(4):
                s = tabs[1, (xd * 4 + yo) * 4 + r]
                piece = cv[s, 16:32]
                if d:
                    sb[1, d, yo, r] = piece
                else:
                    qv[1, x, yo, r] = piece
        if d:
            q1.append(send(sb.at[1, d], qv.at[1, x], xdev(d), sq.at[1, d], rq.at[1, d]))

    for cp in gb:
        cp.wait_recv()
    for h in range(2):
        gcs[4 * h : 4 * h + 4] = (gbr[h, 0] + gbr[h, 1]) + (gbr[h, 2] + gbr[h, 3])
    gc = [send(gcs.at[at_z(d)], gcr.at[z], zdev(d), sgw.at[d], rgw.at[d]) for d in FAR]
    gcr[z] = gcs[z]
    for cp in gc:
        cp.wait_recv()
    total = gcr[0]
    for q in range(1, 8):
        total = total + gcr[q]
    ger[x, y] = total
    gy = [send(ger.at[x, y], ger.at[x, y], ydev(d), sge.at[0, d], rge.at[0, d]) for d in (2, 1, 3)]

    for cp in q0:
        cp.wait_recv()
    e0, e1 = [], []
    for d in (2, 1, 3, 0):
        xd = at_x(d)
        total = [jnp.zeros((16, 128), F32) for _ in range(8)]
        for src in range(4):
            for r in range(4):
                w = tabrs[0, src, 2, (xd * 4 + y) * 4 + r]
                piece = qv[0, src, xd, r]
                for i in range(8):
                    total[i] = total[i] + jnp.where(w == i, 1.0, 0.0).astype(F32) * piece
        for i in range(8):
            if d:
                dv[0, d, i] = total[i]
            else:
                ev[0, x, i] = total[i]
        if d:
            e0.append(send(dv.at[0, d], ev.at[0, x], xdev(d), se.at[0, d], re.at[0, d]))
    for cp in q1:
        cp.wait_recv()
    for d in (2, 1, 3, 0):
        yd = at_y(d)
        total = [jnp.zeros((16, 128), F32) for _ in range(8)]
        for src in range(4):
            for r in range(4):
                w = tabrs[1, src, 2, (x * 4 + yd) * 4 + r]
                piece = qv[1, src, yd, r]
                for i in range(8):
                    total[i] = total[i] + jnp.where(w == i, 1.0, 0.0).astype(F32) * piece
        for i in range(8):
            if d:
                dv[1, d, i] = total[i]
            else:
                ev[1, y, i] = total[i]
        if d:
            e1.append(send(dv.at[1, d], ev.at[1, y], ydev(d), se.at[1, d], re.at[1, d]))

    for cp in gy:
        cp.wait_recv()
    gx = [send(ger.at[x], ger.at[x], xdev(d), sge.at[1, d], rge.at[1, d]) for d in (2, 1, 3)]
    for cp in oz:
        cp.wait_recv()
    for b in range(8):
        out[:, 128 * b : 128 * b + 128] = orv[b]
    for cp in e0 + e1:
        cp.wait_recv()
    for h in range(2):
        for w in range(8):
            gf[16 * h : 16 * h + 16, 128 * w : 128 * w + 128] = (ev[h, 0, w] + ev[h, 1, w]) + (
                ev[h, 2, w] + ev[h, 3, w]
            )
    for cp in gx:
        cp.wait_recv()
    for a in range(4):
        for g in range(4):
            gwt[8 * a : 8 * a + 8, 128 * g : 128 * g + 128] = ger[a, g]
    for cp in pending:
        cp.wait_send()


def hand_over(a, b, c, out, gf, gwt, va, vb, vc, sem):
    trips = ((a, va, out), (b, vb, gf), (c, vc, gwt))
    inward = [pltpu.make_async_copy(src, via, sem.at[0, i]) for i, (src, via, _) in enumerate(trips)]
    outward = [pltpu.make_async_copy(via, dst, sem.at[1, i]) for i, (_, via, dst) in enumerate(trips)]
    for cp in inward:
        cp.start()
    for first, second in zip(inward, outward):
        first.wait()
        second.start()
    for cp in outward:
        cp.wait()


def on_device(feats_t, weight, cot_t, tiles, col_ids, counts):
    vmem = pl.BlockSpec(memory_space=pltpu.VMEM)
    hbm = pl.BlockSpec(memory_space=pltpu.HBM)

    def v(*shape):
        return pltpu.VMEM(shape, F32)

    def dma(*shape):
        return pltpu.SemaphoreType.DMA(shape)

    scratch = [
        v(8, 8, 128, 128),
        pltpu.VMEM((8, 4, 256, 256), BF16),
        v(8, 32, 128),
        v(4, 8, 16, 128),
        v(4, 8, 16, 128),
        v(2, 4, 4, 4, 16, 128),
        v(4, 4, 4, 32, 128),
        v(8, 32, 128),
        v(8, 2, 32, 128),
        v(8, 32, 512),
        pltpu.VMEM((512, 512), BF16),
        pltpu.VMEM((1024, 256), BF16),
        v(8, 32, 128),
        v(8, 32, 128),
        v(8, 32, 128),
        v(8, 2, 32, 128),
        v(8, 32, 128),
        v(8, 32, 128),
        v(8, 32, 128),
        v(4, 4, 4, 8, 128),
        v(4, 4, 4, 8, 128),
        v(4, 4, 4, 8, 128),
        v(4, 4, 4, 8, 128),
        v(2, 4, 4, 8, 128),
        v(2, 4, 4, 8, 128),
        v(8, 8, 128),
        v(8, 8, 128),
        v(4, 4, 8, 128),
        v(64, 32, 128),
        v(2, 4, 4, 4, 16, 128),
        v(2, 4, 4, 4, 16, 128),
        v(2, 4, 8, 16, 128),
        v(2, 4, 8, 16, 128),
        pltpu.VMEM((8, 128), I32),
        pltpu.VMEM((2, 4, 8, 128), I32),
        pltpu.SMEM((8, 128), I32),
        pltpu.SMEM((2, 4, 8, 128), I32),
        pltpu.SMEM((8, 8), I32),
        pltpu.SMEM((8,), I32),
        dma(8), dma(2), dma(12),
        dma(2, 4), dma(2, 4), dma(2, 4), dma(2, 4), dma(2, 4), dma(2, 4),
        dma(8), dma(8), dma(8), dma(8), dma(8), dma(8), dma(8), dma(8),
        pltpu.SemaphoreType.DMA, pltpu.SemaphoreType.DMA,
        dma(8), dma(8), dma(8), dma(8), dma(8), dma(8),
        dma(2, 4), dma(2, 4), dma(2, 4), dma(2, 4),
        dma(2, 4), dma(2, 4), dma(2, 4), dma(2, 4), dma(2, 4), dma(2, 4),
    ]
    out, gf, gwt = pl.pallas_call(
        kernel,
        out_shape=(
            jax.ShapeDtypeStruct((32, 1024), F32),
            jax.ShapeDtypeStruct((32, 1024), F32),
            jax.ShapeDtypeStruct((32, 512), F32),
        ),
        in_specs=[hbm] * 6,
        out_specs=(vmem, vmem, vmem),
        scratch_shapes=scratch,
        name="graph_layer",
        cost_estimate=pl.CostEstimate(flops=10**9, bytes_accessed=6 * 10**6, transcendentals=32768),
        compiler_params=pltpu.CompilerParams(
            collective_id=0, has_side_effects=True, vmem_limit_bytes=61936 * 1024
        ),
    )(feats_t, weight.T, cot_t, tiles, col_ids, counts)
    anywhere = pl.BlockSpec(memory_space=pl.ANY)
    out, gf, gwt = pl.pallas_call(
        hand_over,
        out_shape=(
            jax.ShapeDtypeStruct((32, 1024), F32),
            jax.ShapeDtypeStruct((32, 1024), F32),
            jax.ShapeDtypeStruct((32, 512), F32),
        ),
        in_specs=[anywhere] * 3,
        out_specs=(anywhere,) * 3,
        scratch_shapes=[v(32, 1024), v(32, 1024), v(32, 512), dma(2, 3)],
        name="hand_over",
        cost_estimate=pl.CostEstimate(flops=0, bytes_accessed=2 * 320 * 1024, transcendentals=0),
    )(out, gf, gwt)
    return out, gf, gwt.T


def solution(mesh):
    return jax.shard_map(
        on_device,
        mesh=mesh,
        in_specs=(
            P("feat", "node"),
            P(None, "feat"),
            P("feat", "node"),
            P("node", None, None, None),
            P("node", None),
            P("node"),
        ),
        out_specs=(P("feat", "node"), P("feat", "node"), P(None, "feat")),
        check_vma=False,
    )
```

```python
import jax
import jax.numpy as jnp
from jax import lax
from jax.experimental import pallas as pl
from jax.experimental.pallas import tpu as pltpu
from jax.sharding import PartitionSpec as P

MESH = pl.DeviceIdType.MESH
F32 = jnp.float32
BF16 = jnp.bfloat16
I32 = jnp.int32
NN = (((1,), (0,)), ((), ()))
NT = (((1,), (1,)), ((), ()))
FAR = (4, 3, 5, 2, 6, 1, 7)
PLANE = sorted(((i, j) for i in range(4) for j in range(4) if i + j), key=lambda d: -min(d[0], 4 - d[0]) - min(d[1], 4 - d[1]))


def split(v):
    hi = v.astype(BF16)
    return hi, (v - hi.astype(F32)).astype(BF16)


def mm(a, b, dims):
    return lax.dot_general(a, b, dims, preferred_element_type=F32)


def kernel(
    feats, wt, cot, tiles, cols_h, counts_h,
    out, gf, gwt,
    t32, tb, fo, a01, a02, a03, a11, a12, a13, sv, rv, mx, mv, wa, wst, wn, ca,
    oo, orv, pv, px, gs, gv, wp, gar, gcs, gcr, ger,
    cv, sb, qv, dv, ev, tab, tabr, tabs, tabrs, cols, counts,
    sem_t, sem_s, sem_i,
    s1, r1, s1t, r1t, s2, r2, sw, rw, sc, rc, sm, rm, sf, rf, sp, rp,
    so, ro, sg, rg, sgw, rgw, sq, rq, se, re, sga, rga, sge, rge,
):
    node = lax.axis_index("node")
    feat = lax.axis_index("feat")
    x, y = lax.div(node, 4), lax.rem(node, 4)
    z, c = lax.div(feat, 2), lax.rem(feat, 2)
    oc = 1 - c

    def at_x(d):
        return lax.rem(x + d, 4)

    def at_y(d):
        return lax.rem(y + d, 4)

    def at_z(d):
        return lax.rem(z + d, 8)

    def xdev(d):
        return (at_x(d) * 4 + y, feat)

    def ydev(d):
        return (x * 4 + at_y(d), feat)

    def xydev(dx, dy):
        return (at_x(dx) * 4 + at_y(dy), feat)

    def zdev(d):
        return (node, at_z(d) * 2 + c)

    cdev = (node, z * 2 + oc)
    pending = []

    def send(src, dst, device, ss, rs):
        cp = pltpu.make_async_remote_copy(
            src_ref=src, dst_ref=dst, send_sem=ss, recv_sem=rs,
            device_id=device, device_id_type=MESH,
        )
        cp.start()
        pending.append(cp)
        return cp

    ids = [
        pltpu.make_async_copy(cols_h, cols, sem_i.at[0]),
        pltpu.make_async_copy(counts_h, counts, sem_i.at[1]),
    ]
    fcopies = [
        pltpu.make_async_copy(feats.at[:, pl.ds(128 * w, 128)], fo.at[w], sem_i.at[2 + w])
        for w in range(8)
    ]
    own = [
        pltpu.make_async_copy(wt, wa.at[z], sem_i.at[10]),
        pltpu.make_async_copy(cot.at[:, pl.ds(pl.multiple_of(z * 128, 128), 128)], ca.at[z], sem_i.at[11]),
    ]
    for cp in fcopies + ids + own:
        cp.start()
    for b in range(8):
        pltpu.make_async_copy(tiles.at[b], t32.at[b], sem_t.at[b]).start()
    barrier = pltpu.get_barrier_semaphore()
    peers = [zdev(d) for d in (4, 3, 5, 2, 6, 1, 7)] + [xydev(*d) for d in PLANE] + [cdev]
    for p in peers:
        pl.semaphore_signal(barrier, 1, device_id=p, device_id_type=MESH)

    for cp in fcopies:
        cp.wait()
    pl.semaphore_wait(barrier, len(peers))

    heard = ((None, a01, a02, a03), (None, a11, a12, a13))
    fx, fy = {}, {}
    for d in (1, 3, 2):
        fx[d] = send(fo.at[:, pl.ds(0, 16)], heard[0][d], xdev(d), s1.at[0, d], r1.at[0, d])
        fy[d] = send(fo.at[:, pl.ds(16, 16)], heard[1][d], ydev(d), s1.at[1, d], r1.at[1, d])

    for cp in ids:
        cp.wait()
    lane8 = lax.broadcasted_iota(I32, (8, 128), 1)
    sub8 = lax.broadcasted_iota(I32, (8, 128), 0)
    by_lane = jnp.full((8, 128), 1024, I32)
    for s in range(64):
        by_lane = jnp.where(lane8 == s, cols[s // 8, s % 8], by_lane)
    place_l = jnp.zeros((8, 128), I32)
    rows = []
    for g in range(8):
        by_sub = jnp.zeros((8, 128), I32)
        for k in range(8):
            by_sub = jnp.where(sub8 == k, cols[g, k], by_sub)
        rows.append(by_sub)
    own_l = lax.shift_right_logical(by_lane, 3)
    slot_sum = jnp.zeros((8, 128), I32)
    want_sum = jnp.zeros((8, 128), I32)
    for g in range(8):
        own_s = lax.shift_right_logical(rows[g], 3)
        slot_s = sub8 + 8 * g
        same = own_s == own_l
        place_l = place_l + jnp.where(same & (slot_s < lane8), 1, 0)
        rank = jnp.sum(jnp.where(same & (lane8 < slot_s), 1, 0), axis=1, keepdims=True)
        hit = (own_s * 4 + rank) == lane8
        slot_sum = slot_sum + jnp.where(hit, slot_s, 0)
        want_sum = want_sum + jnp.where(hit, rows[g] & 7, 0)
    place = own_l * 4 + jnp.sum(place_l, axis=0, keepdims=True)
    slot_of = jnp.sum(slot_sum, axis=0, keepdims=True)
    want = jnp.sum(want_sum, axis=0, keepdims=True)
    table = jnp.where(sub8 == 0, place, jnp.where(sub8 == 1, slot_of, want))
    tab[...] = table
    tabr[0, y] = table
    tabr[1, x] = table

    tx = [send(tab, tabr.at[1, x], xdev(d), s1t.at[0, d], r1t.at[0, d]) for d in (1, 2, 3)]
    ty = [send(tab, tabr.at[0, y], ydev(d), s1t.at[1, d], r1t.at[1, d]) for d in (1, 2, 3)]
    to_s = pltpu.make_async_copy(tab, tabs, sem_s.at[0])
    to_s.start()
    cz = [send(cot.at[:, pl.ds(pl.multiple_of(at_z(d) * 128, 128), 128)], ca.at[z], zdev(d), sc.at[d], rc.at[d]) for d in FAR]
    wz = [send(wt, wa.at[z], zdev(d), sw.at[d], rw.at[d]) for d in FAR]
    to_s.wait()
    for cp in tx + ty:
        cp.wait_recv()
    to_rs = pltpu.make_async_copy(tabr, tabrs, sem_s.at[1])
    to_rs.start()
    to_rs.wait()

    leg2 = []
    for g in (0, 1, 3, 2):
        for h in range(2):
            if g:
                (fx, fy)[h][g].wait_recv()
            xo, yo = at_x(4 - g), at_y(4 - g)
            for d in (2, 1, 3, 0):
                for r in range(4):
                    if h == 0:
                        w = tabrs[0, at_y(d), 2, (xo * 4 + y) * 4 + r]
                    else:
                        w = tabrs[1, at_x(d), 2, (x * 4 + yo) * 4 + r]
                    block = heard[h][g][w] if g else fo[w, 16 * h : 16 * h + 16]
                    if d:
                        sv[h, g, d, r] = block
                    elif h == 0:
                        rv[xo, y, r, 0:16] = block
                    else:
                        rv[x, yo, r, 16:32] = block
                if d and h == 0:
                    to = rv.at[xo, y, :, pl.ds(0, 16)]
                    leg2.append(send(sv.at[0, g, d], to, ydev(d), s2.at[0, g, d], r2.at[0, g, d]))
                elif d:
                    to = rv.at[x, yo, :, pl.ds(16, 16)]
                    leg2.append(send(sv.at[1, g, d], to, xdev(d), s2.at[1, g, d], r2.at[1, g, d]))

    def convert(b, carry):
        pltpu.make_async_copy(tiles.at[b], t32.at[b], sem_t.at[b]).wait()
        for k in range(8):
            live = jnp.where(k < counts[b], 1.0, 0.0).astype(F32)
            hi, lo = split(t32[b, k] * live)
            q = 128 * (k % 2)
            tb[b, k // 2, 0:128, q : q + 128] = hi
            tb[b, k // 2, 128:256, q : q + 128] = lo
        return carry

    lax.fori_loop(0, 8, convert, 0)

    for cp in leg2:
        cp.wait_recv()

    mz = []
    for d in FAR + (0,):
        b = at_z(d)
        acc = None
        for kp in range(4):
            parts = []
            for k in (2 * kp, 2 * kp + 1):
                p = tabs[0, b * 8 + k]
                parts.append(
                    split(rv[lax.shift_right_logical(p, 4), lax.shift_right_logical(p, 2) & 3, p & 3])
                )
            lhs = jnp.concatenate(
                [
                    jnp.concatenate([parts[0][0], parts[1][0]], axis=1),
                    jnp.concatenate([parts[0][1], parts[1][1]], axis=1),
                ],
                axis=0,
            )
            term = mm(lhs, tb[b, kp], NT)
            acc = term if acc is None else acc + term
        mixed = (acc[32:64, 128:256] + acc[32:64, 0:128] + acc[0:32, 128:256]) + acc[0:32, 0:128]
        if d:
            mx[d] = mixed
            mz.append(send(mx.at[d], mv.at[z, c], zdev(d), sm.at[d], rm.at[d]))
        else:
            mv[z, c] = mixed
    for cp in wz:
        cp.wait_recv()
    for cp in own:
        cp.wait()
    for q in range(8):
        hi, lo = split(wa[q])
        wst[32 * q : 32 * q + 32] = hi
        wst[256 + 32 * q : 288 + 32 * q] = lo
    for g in range(4):
        turned = jnp.transpose(wa[:, :, 128 * g : 128 * g + 128].reshape(256, 128))
        hi, lo = split(turned)
        wn[128 * g : 128 * g + 128] = hi
        wn[512 + 128 * g : 640 + 128 * g] = lo

    fz = [send(mv.at[z, c], mv.at[z, c], cdev, sf.at[0], rf.at[0])]
    for i, d in enumerate(FAR):
        mz[i].wait_recv()
        q = at_z(8 - d)
        fz.append(send(mv.at[q, c], mv.at[q, c], cdev, sf.at[d], rf.at[d]))
    for cp in cz:
        cp.wait_recv()
    for cp in fz:
        cp.wait_recv()

    hi, lo = split(mv[...].reshape(512, 128))
    mhl = jnp.concatenate([hi, lo], axis=1)
    r = mm(wst[...], mhl, NN)
    pre = (r[256:512, 128:256] + r[256:512, 0:128] + r[0:256, 128:256]) + r[0:256, 0:128]
    sig = jax.nn.sigmoid(pre)
    gp = ca[...].reshape(256, 128) * (sig * (1.0 + pre * (1.0 - sig)))
    ghi, glo = split(gp)
    r = mm(wn[...], jnp.concatenate([ghi, glo], axis=1), NN)
    part = (r[512:1024, 128:256] + r[512:1024, 0:128] + r[0:512, 128:256]) + r[0:512, 0:128]
    pv[...] = part.reshape(8, 2, 32, 128)
    xc = send(pv.at[:, oc], px, cdev, sp, rp)
    oo[...] = (pre * sig).reshape(8, 32, 128)
    g2 = jnp.concatenate(
        [jnp.concatenate([ghi, ghi], axis=1), jnp.concatenate([glo, glo], axis=1)], axis=0
    )
    r = mm(g2, mhl, NT)
    r = r[0:256] + r[256:512]
    for q in range(8):
        for a in range(4):
            for g in range(4):
                chunk = r[32 * q + 8 * a : 32 * q + 8 * a + 8, 128 * g : 128 * g + 128]
                wp[a, g, q] = chunk
    xc.wait_recv()
    gz = []
    gs[...] = pv[:, c] + px[...]
    for d in FAR:
        gz.append(send(gs.at[at_z(d)], gv.at[z], zdev(d), sg.at[d], rg.at[d]))
    gv[z] = gs[z]
    ga = [
        send(wp.at[at_x(i), at_y(j)], gar.at[x, y], xydev(i, j), sga.at[i, j], rga.at[i, j])
        for i, j in PLANE
    ]
    gar[x, y] = wp[x, y]
    oz = [send(oo.at[at_z(d)], orv.at[z], zdev(d), so.at[d], ro.at[d]) for d in FAR]
    orv[z] = oo[z]

    arrivals = {d: cp for d, cp in zip(FAR, gz)}
    for d in (0, 1, 7, 2, 6, 3, 5, 4):
        if d:
            arrivals[d].wait_recv()
        b = at_z(8 - d)
        ghi, glo = split(gv[b])
        lhs = jnp.concatenate(
            [jnp.concatenate([ghi, ghi], axis=1), jnp.concatenate([glo, glo], axis=1)], axis=0
        )
        for kp in range(4):
            r = mm(lhs, tb[b, kp], NN)
            r = r[0:32] + r[32:64]
            cv[b * 8 + 2 * kp] = r[:, 0:128]
            cv[b * 8 + 2 * kp + 1] = r[:, 128:256]

    back = {}
    for g in (2, 1, 3, 0):
        for h in range(2):
            for d in (2, 1, 3, 0):
                for r in range(4):
                    if h == 0:
                        s = tabs[1, (at_x(g) * 4 + at_y(d)) * 4 + r]
                    else:
                        s = tabs[1, (at_x(d) * 4 + at_y(g)) * 4 + r]
                    piece = cv[s, 16 * h : 16 * h + 16]
                    if d:
                        sb[h, g, d, r] = piece
                    elif h == 0:
                        qv[0, g, y, r] = piece
                    else:
                        qv[1, g, x, r] = piece
                if d and h == 0:
                    to = qv.at[0, g, y]
                    back[h, g, d] = send(sb.at[0, g, d], to, ydev(d), sq.at[0, g, d], rq.at[0, g, d])
                elif d:
                    to = qv.at[1, g, x]
                    back[h, g, d] = send(sb.at[1, g, d], to, xdev(d), sq.at[1, g, d], rq.at[1, g, d])

    for cp in ga:
        cp.wait_recv()
    held = gar[0, 0]
    for q in range(1, 16):
        held = held + gar[q // 4, q % 4]
    gcs[...] = held
    gc = [send(gcs.at[at_z(d)], gcr.at[z], zdev(d), sgw.at[d], rgw.at[d]) for d in FAR]
    gcr[z] = gcs[z]

    last = []
    for g in (2, 1, 3, 0):
        for h in range(2):
            for d in (1, 3, 2):
                back[h, g, d].wait_recv()
            total = [jnp.zeros((16, 128), F32) for _ in range(8)]
            for src in range(4):
                for r in range(4):
                    if h == 0:
                        w = tabrs[0, src, 2, (at_x(g) * 4 + y) * 4 + r]
                    else:
                        w = tabrs[1, src, 2, (x * 4 + at_y(g)) * 4 + r]
                    piece = qv[h, g, src, r]
                    for i in range(8):
                        total[i] = total[i] + jnp.where(w == i, 1.0, 0.0).astype(F32) * piece
            for i in range(8):
                if g:
                    dv[h, g, i] = total[i]
                else:
                    ev[h, 0, i] = total[i]
            if g:
                device = ydev(g) if h else xdev(g)
                last.append(send(dv.at[h, g], ev.at[h, g], device, se.at[h, g], re.at[h, g]))

        if g == 1:
            for cp in gc:
                cp.wait_recv()
            held = gcr[0]
            for q in range(1, 8):
                held = held + gcr[q]
            ger[x, y] = held
            ge = [
                send(ger.at[x, y], ger.at[x, y], xydev(i, j), sge.at[i, j], rge.at[i, j])
                for i, j in PLANE
            ]

    for cp in oz:
        cp.wait_recv()
    for b in range(8):
        out[:, 128 * b : 128 * b + 128] = orv[b]
    for cp in last:
        cp.wait_recv()
    for h in range(2):
        for w in range(8):
            gf[16 * h : 16 * h + 16, 128 * w : 128 * w + 128] = (ev[h, 0, w] + ev[h, 1, w]) + (
                ev[h, 2, w] + ev[h, 3, w]
            )
    for cp in ge:
        cp.wait_recv()
    for a in range(4):
        for g in range(4):
            gwt[8 * a : 8 * a + 8, 128 * g : 128 * g + 128] = ger[a, g]
    for cp in pending:
        cp.wait_send()


def hand_over(a, b, c, out, gf, gwt, va, vb, vc, sem):
    trips = ((a, va, out), (b, vb, gf), (c, vc, gwt))
    inward = [pltpu.make_async_copy(src, via, sem.at[0, i]) for i, (src, via, _) in enumerate(trips)]
    outward = [pltpu.make_async_copy(via, dst, sem.at[1, i]) for i, (_, via, dst) in enumerate(trips)]
    for cp in inward:
        cp.start()
    for first, second in zip(inward, outward):
        first.wait()
        second.start()
    for cp in outward:
        cp.wait()


def on_device(feats_t, weight, cot_t, tiles, col_ids, counts):
    vmem = pl.BlockSpec(memory_space=pltpu.VMEM)
    hbm = pl.BlockSpec(memory_space=pltpu.HBM)

    def v(*shape):
        return pltpu.VMEM(shape, F32)

    def dma(*shape):
        return pltpu.SemaphoreType.DMA(shape)

    scratch = [
        v(8, 8, 128, 128),
        pltpu.VMEM((8, 4, 256, 256), BF16),
        v(8, 32, 128),
        v(8, 16, 128), v(8, 16, 128), v(8, 16, 128),
        v(8, 16, 128), v(8, 16, 128), v(8, 16, 128),
        v(2, 4, 4, 4, 16, 128),
        v(4, 4, 4, 32, 128),
        v(8, 32, 128),
        v(8, 2, 32, 128),
        v(8, 32, 512),
        pltpu.VMEM((512, 512), BF16),
        pltpu.VMEM((1024, 256), BF16),
        v(8, 32, 128),
        v(8, 32, 128),
        v(8, 32, 128),
        v(8, 2, 32, 128),
        v(8, 32, 128),
        v(8, 32, 128),
        v(8, 32, 128),
        v(4, 4, 8, 8, 128),
        v(4, 4, 8, 8, 128),
        v(8, 8, 128),
        v(8, 8, 128),
        v(4, 4, 8, 128),
        v(64, 32, 128),
        v(2, 4, 4, 4, 16, 128),
        v(2, 4, 4, 4, 16, 128),
        v(2, 4, 8, 16, 128),
        v(2, 4, 8, 16, 128),
        pltpu.VMEM((8, 128), I32),
        pltpu.VMEM((2, 4, 8, 128), I32),
        pltpu.SMEM((8, 128), I32),
        pltpu.SMEM((2, 4, 8, 128), I32),
        pltpu.SMEM((8, 8), I32),
        pltpu.SMEM((8,), I32),
        dma(8), dma(2), dma(12),
        dma(2, 4), dma(2, 4), dma(2, 4), dma(2, 4), dma(2, 4, 4), dma(2, 4, 4),
        dma(8), dma(8), dma(8), dma(8), dma(8), dma(8), dma(8), dma(8),
        pltpu.SemaphoreType.DMA, pltpu.SemaphoreType.DMA,
        dma(8), dma(8), dma(8), dma(8), dma(8), dma(8),
        dma(2, 4, 4), dma(2, 4, 4), dma(2, 4), dma(2, 4),
        dma(4, 4), dma(4, 4), dma(4, 4), dma(4, 4),
    ]
    out, gf, gwt = pl.pallas_call(
        kernel,
        out_shape=(
            jax.ShapeDtypeStruct((32, 1024), F32),
            jax.ShapeDtypeStruct((32, 1024), F32),
            jax.ShapeDtypeStruct((32, 512), F32),
        ),
        in_specs=[hbm] * 6,
        out_specs=(vmem, vmem, vmem),
        scratch_shapes=scratch,
        name="graph_layer",
        cost_estimate=pl.CostEstimate(flops=10**9, bytes_accessed=6 * 10**6, transcendentals=32768),
        compiler_params=pltpu.CompilerParams(
            collective_id=0, has_side_effects=True, vmem_limit_bytes=61936 * 1024
        ),
    )(feats_t, weight.T, cot_t, tiles, col_ids, counts)
    anywhere = pl.BlockSpec(memory_space=pl.ANY)
    out, gf, gwt = pl.pallas_call(
        hand_over,
        out_shape=(
            jax.ShapeDtypeStruct((32, 1024), F32),
            jax.ShapeDtypeStruct((32, 1024), F32),
            jax.ShapeDtypeStruct((32, 512), F32),
        ),
        in_specs=[anywhere] * 3,
        out_specs=(anywhere,) * 3,
        scratch_shapes=[v(32, 1024), v(32, 1024), v(32, 512), dma(2, 3)],
        name="hand_over",
        cost_estimate=pl.CostEstimate(flops=0, bytes_accessed=2 * 320 * 1024, transcendentals=0),
    )(out, gf, gwt)
    return out, gf, gwt.T


def solution(mesh):
    return jax.shard_map(
        on_device,
        mesh=mesh,
        in_specs=(
            P("feat", "node"),
            P(None, "feat"),
            P("feat", "node"),
            P("node", None, None, None),
            P("node", None),
            P("node"),
        ),
        out_specs=(P("feat", "node"), P("feat", "node"), P(None, "feat")),
        check_vma=False,
    )
```

```python
import jax
import jax.numpy as jnp
from jax import lax
from jax.experimental import pallas as pl
from jax.experimental.pallas import tpu as pltpu
from jax.sharding import PartitionSpec as P

MESH = pl.DeviceIdType.MESH
F32 = jnp.float32
BF16 = jnp.bfloat16
I32 = jnp.int32
NN = (((1,), (0,)), ((), ()))
NT = (((1,), (1,)), ((), ()))
FAR = (4, 3, 5, 2, 6, 1, 7)
PLANE = sorted(((i, j) for i in range(4) for j in range(4) if i + j), key=lambda d: -min(d[0], 4 - d[0]) - min(d[1], 4 - d[1]))


def split(v):
    hi = v.astype(BF16)
    return hi, (v - hi.astype(F32)).astype(BF16)


def mm(a, b, dims):
    return lax.dot_general(a, b, dims, preferred_element_type=F32)


def kernel(
    feats, wt, cot, tiles, cols_h, counts_h,
    out, gf, gwt,
    t32, tb, fo, a01, a02, a03, a11, a12, a13, sv, rv, mx, mv, wa, wst, wn, ca,
    oo, orv, pv, px, gs, gv, wp, gar, gcs, gcr, ger,
    cv, sb, qv, dv, ev, tab, tabr, tabs, tabrs, cols, counts,
    sem_t, sem_s, sem_i,
    s1, r1, s1t, r1t, s2, r2, sw, rw, sc, rc, sm, rm, sf, rf, sp, rp,
    so, ro, sg, rg, sgw, rgw, sq, rq, se, re, sga, rga, sge, rge,
):
    node = lax.axis_index("node")
    feat = lax.axis_index("feat")
    x, y = lax.div(node, 4), lax.rem(node, 4)
    z, c = lax.div(feat, 2), lax.rem(feat, 2)
    oc = 1 - c

    def at_x(d):
        return lax.rem(x + d, 4)

    def at_y(d):
        return lax.rem(y + d, 4)

    def at_z(d):
        return lax.rem(z + d, 8)

    def xdev(d):
        return (at_x(d) * 4 + y, feat)

    def ydev(d):
        return (x * 4 + at_y(d), feat)

    def xydev(dx, dy):
        return (at_x(dx) * 4 + at_y(dy), feat)

    def zdev(d):
        return (node, at_z(d) * 2 + c)

    cdev = (node, z * 2 + oc)
    pending = []

    def send(src, dst, device, ss, rs):
        cp = pltpu.make_async_remote_copy(
            src_ref=src, dst_ref=dst, send_sem=ss, recv_sem=rs,
            device_id=device, device_id_type=MESH,
        )
        cp.start()
        pending.append(cp)
        return cp

    ids = [
        pltpu.make_async_copy(cols_h, cols, sem_i.at[0]),
        pltpu.make_async_copy(counts_h, counts, sem_i.at[1]),
    ]
    fcopies = [
        pltpu.make_async_copy(feats.at[:, pl.ds(128 * w, 128)], fo.at[w], sem_i.at[2 + w])
        for w in range(8)
    ]
    own = [
        pltpu.make_async_copy(wt, wa.at[z], sem_i.at[10]),
        pltpu.make_async_copy(cot.at[:, pl.ds(pl.multiple_of(z * 128, 128), 128)], ca.at[z], sem_i.at[11]),
    ]
    for cp in fcopies + ids + own:
        cp.start()
    for b in range(8):
        pltpu.make_async_copy(tiles.at[b], t32.at[b], sem_t.at[b]).start()
    barrier = pltpu.get_barrier_semaphore()
    peers = [zdev(d) for d in (4, 3, 5, 2, 6, 1, 7)] + [xydev(*d) for d in PLANE] + [cdev]
    for p in peers:
        pl.semaphore_signal(barrier, 1, device_id=p, device_id_type=MESH)

    for cp in ids:
        cp.wait()
    lane8 = lax.broadcasted_iota(I32, (8, 128), 1)
    sub8 = lax.broadcasted_iota(I32, (8, 128), 0)
    by_lane = jnp.full((8, 128), 1024, I32)
    for s in range(64):
        by_lane = jnp.where(lane8 == s, cols[s // 8, s % 8], by_lane)
    place_l = jnp.zeros((8, 128), I32)
    rows = []
    for g in range(8):
        by_sub = jnp.zeros((8, 128), I32)
        for k in range(8):
            by_sub = jnp.where(sub8 == k, cols[g, k], by_sub)
        rows.append(by_sub)
    own_l = lax.shift_right_logical(by_lane, 3)
    slot_sum = jnp.zeros((8, 128), I32)
    want_sum = jnp.zeros((8, 128), I32)
    for g in range(8):
        own_s = lax.shift_right_logical(rows[g], 3)
        slot_s = sub8 + 8 * g
        same = own_s == own_l
        place_l = place_l + jnp.where(same & (slot_s < lane8), 1, 0)
        rank = jnp.sum(jnp.where(same & (lane8 < slot_s), 1, 0), axis=1, keepdims=True)
        hit = (own_s * 4 + rank) == lane8
        slot_sum = slot_sum + jnp.where(hit, slot_s, 0)
        want_sum = want_sum + jnp.where(hit, rows[g] & 7, 0)
    place = own_l * 4 + jnp.sum(place_l, axis=0, keepdims=True)
    slot_of = jnp.sum(slot_sum, axis=0, keepdims=True)
    want = jnp.sum(want_sum, axis=0, keepdims=True)
    table = jnp.where(sub8 == 0, place, jnp.where(sub8 == 1, slot_of, want))
    tab[...] = table
    tabr[0, y] = table
    tabr[1, x] = table
    for cp in fcopies:
        cp.wait()
    pl.semaphore_wait(barrier, len(peers))

    heard = ((None, a01, a02, a03), (None, a11, a12, a13))
    fx, fy = {}, {}
    for d in (1, 3, 2):
        fx[d] = send(fo.at[:, pl.ds(0, 16)], heard[0][d], xdev(d), s1.at[0, d], r1.at[0, d])
        fy[d] = send(fo.at[:, pl.ds(16, 16)], heard[1][d], ydev(d), s1.at[1, d], r1.at[1, d])

    tx = [send(tab, tabr.at[1, x], xdev(d), s1t.at[0, d], r1t.at[0, d]) for d in (1, 2, 3)]
    ty = [send(tab, tabr.at[0, y], ydev(d), s1t.at[1, d], r1t.at[1, d]) for d in (1, 2, 3)]
    to_s = pltpu.make_async_copy(tab, tabs, sem_s.at[0])
    to_s.start()
    cz = [send(cot.at[:, pl.ds(pl.multiple_of(at_z(d) * 128, 128), 128)], ca.at[z], zdev(d), sc.at[d], rc.at[d]) for d in FAR]
    wz = [send(wt, wa.at[z], zdev(d), sw.at[d], rw.at[d]) for d in FAR]
    to_s.wait()
    for cp in tx + ty:
        cp.wait_recv()
    to_rs = pltpu.make_async_copy(tabr, tabrs, sem_s.at[1])
    to_rs.start()
    to_rs.wait()

    leg2 = []
    for g in (0, 1, 3, 2):
        for h in range(2):
            if g:
                (fx, fy)[h][g].wait_recv()
            xo, yo = at_x(4 - g), at_y(4 - g)
            for d in (2, 1, 3, 0):
                for r in range(4):
                    if h == 0:
                        w = tabrs[0, at_y(d), 2, (xo * 4 + y) * 4 + r]
                    else:
                        w = tabrs[1, at_x(d), 2, (x * 4 + yo) * 4 + r]
                    block = heard[h][g][w] if g else fo[w, 16 * h : 16 * h + 16]
                    if d:
                        sv[h, g, d, r] = block
                    elif h == 0:
                        rv[xo, y, r, 0:16] = block
                    else:
                        rv[x, yo, r, 16:32] = block
                if d and h == 0:
                    to = rv.at[xo, y, :, pl.ds(0, 16)]
                    leg2.append(send(sv.at[0, g, d], to, ydev(d), s2.at[0, g, d], r2.at[0, g, d]))
                elif d:
                    to = rv.at[x, yo, :, pl.ds(16, 16)]
                    leg2.append(send(sv.at[1, g, d], to, xdev(d), s2.at[1, g, d], r2.at[1, g, d]))

    def convert(b, carry):
        pltpu.make_async_copy(tiles.at[b], t32.at[b], sem_t.at[b]).wait()
        for k in range(8):
            live = jnp.where(k < counts[b], 1.0, 0.0).astype(F32)
            hi, lo = split(t32[b, k] * live)
            q = 128 * (k % 2)
            tb[b, k // 2, 0:128, q : q + 128] = hi
            tb[b, k // 2, 128:256, q : q + 128] = lo
        return carry

    lax.fori_loop(0, 8, convert, 0)

    for cp in leg2:
        cp.wait_recv()

    mz = []
    for d in FAR + (0,):
        b = at_z(d)
        acc = None
        for kp in range(4):
            parts = []
            for k in (2 * kp, 2 * kp + 1):
                p = tabs[0, b * 8 + k]
                parts.append(
                    split(rv[lax.shift_right_logical(p, 4), lax.shift_right_logical(p, 2) & 3, p & 3])
                )
            lhs = jnp.concatenate(
                [
                    jnp.concatenate([parts[0][0], parts[1][0]], axis=1),
                    jnp.concatenate([parts[0][1], parts[1][1]], axis=1),
                ],
                axis=0,
            )
            term = mm(lhs, tb[b, kp], NT)
            acc = term if acc is None else acc + term
        mixed = (acc[32:64, 128:256] + acc[32:64, 0:128] + acc[0:32, 128:256]) + acc[0:32, 0:128]
        if d:
            mx[d] = mixed
            mz.append(send(mx.at[d], mv.at[z, c], zdev(d), sm.at[d], rm.at[d]))
        else:
            mv[z, c] = mixed
    for cp in wz:
        cp.wait_recv()
    for cp in own:
        cp.wait()
    for q in range(8):
        hi, lo = split(wa[q])
        wst[32 * q : 32 * q + 32] = hi
        wst[256 + 32 * q : 288 + 32 * q] = lo
    for g in range(4):
        turned = jnp.transpose(wa[:, :, 128 * g : 128 * g + 128].reshape(256, 128))
        hi, lo = split(turned)
        wn[128 * g : 128 * g + 128] = hi
        wn[512 + 128 * g : 640 + 128 * g] = lo

    fz = [send(mv.at[z, c], mv.at[z, c], cdev, sf.at[0], rf.at[0])]
    for d in (2, 6, 1, 7, 3, 5, 4):
        mz[FAR.index(d)].wait_recv()
        q = at_z(8 - d)
        fz.append(send(mv.at[q, c], mv.at[q, c], cdev, sf.at[d], rf.at[d]))
    for cp in cz:
        cp.wait_recv()
    for cp in fz:
        cp.wait_recv()

    hi, lo = split(mv[...].reshape(512, 128))
    mhl = jnp.concatenate([hi, lo], axis=1)
    r = mm(wst[...], mhl, NN)
    pre = (r[256:512, 128:256] + r[256:512, 0:128] + r[0:256, 128:256]) + r[0:256, 0:128]
    sig = jax.nn.sigmoid(pre)
    gp = ca[...].reshape(256, 128) * (sig * (1.0 + pre * (1.0 - sig)))
    ghi, glo = split(gp)
    r = mm(wn[...], jnp.concatenate([ghi, glo], axis=1), NN)
    part = (r[512:1024, 128:256] + r[512:1024, 0:128] + r[0:512, 128:256]) + r[0:512, 0:128]
    pv[...] = part.reshape(8, 2, 32, 128)
    xc = send(pv.at[:, oc], px, cdev, sp, rp)
    oo[...] = (pre * sig).reshape(8, 32, 128)
    g2 = jnp.concatenate(
        [jnp.concatenate([ghi, ghi], axis=1), jnp.concatenate([glo, glo], axis=1)], axis=0
    )
    r = mm(g2, mhl, NT)
    r = r[0:256] + r[256:512]
    for q in range(8):
        for a in range(4):
            for g in range(4):
                chunk = r[32 * q + 8 * a : 32 * q + 8 * a + 8, 128 * g : 128 * g + 128]
                wp[a, g, q] = chunk
    xc.wait_recv()
    gz = []
    gs[...] = pv[:, c] + px[...]
    for d in FAR:
        gz.append(send(gs.at[at_z(d)], gv.at[z], zdev(d), sg.at[d], rg.at[d]))
    gv[z] = gs[z]
    ga = [
        send(wp.at[at_x(i), at_y(j)], gar.at[x, y], xydev(i, j), sga.at[i, j], rga.at[i, j])
        for i, j in PLANE
    ]
    gar[x, y] = wp[x, y]
    orv[z] = oo[z]

    arrivals = {d: cp for d, cp in zip(FAR, gz)}
    for d in (0, 1, 7, 2, 6, 3, 5, 4):
        if d:
            arrivals[d].wait_recv()
        b = at_z(8 - d)
        ghi, glo = split(gv[b])
        lhs = jnp.concatenate(
            [jnp.concatenate([ghi, ghi], axis=1), jnp.concatenate([glo, glo], axis=1)], axis=0
        )
        for kp in range(4):
            r = mm(lhs, tb[b, kp], NN)
            r = r[0:32] + r[32:64]
            cv[b * 8 + 2 * kp] = r[:, 0:128]
            cv[b * 8 + 2 * kp + 1] = r[:, 128:256]

    back = {}
    for g in (2, 1, 3, 0):
        for h in range(2):
            for d in (2, 1, 3, 0):
                for r in range(4):
                    if h == 0:
                        s = tabs[1, (at_x(g) * 4 + at_y(d)) * 4 + r]
                    else:
                        s = tabs[1, (at_x(d) * 4 + at_y(g)) * 4 + r]
                    piece = cv[s, 16 * h : 16 * h + 16]
                    if d:
                        sb[h, g, d, r] = piece
                    elif h == 0:
                        qv[0, g, y, r] = piece
                    else:
                        qv[1, g, x, r] = piece
                if d and h == 0:
                    to = qv.at[0, g, y]
                    back[h, g, d] = send(sb.at[0, g, d], to, ydev(d), sq.at[0, g, d], rq.at[0, g, d])
                elif d:
                    to = qv.at[1, g, x]
                    back[h, g, d] = send(sb.at[1, g, d], to, xdev(d), sq.at[1, g, d], rq.at[1, g, d])

    oz = [send(oo.at[at_z(d)], orv.at[z], zdev(d), so.at[d], ro.at[d]) for d in FAR]

    for cp in ga:
        cp.wait_recv()
    held = gar[0, 0]
    for q in range(1, 16):
        held = held + gar[q // 4, q % 4]
    gcs[...] = held
    gc = [send(gcs.at[at_z(d)], gcr.at[z], zdev(d), sgw.at[d], rgw.at[d]) for d in FAR]
    gcr[z] = gcs[z]

    last = []
    for g in (2, 1, 3, 0):
        for h in range(2):
            for d in (1, 3, 2):
                back[h, g, d].wait_recv()
            total = [jnp.zeros((16, 128), F32) for _ in range(8)]
            for src in range(4):
                for r in range(4):
                    if h == 0:
                        w = tabrs[0, src, 2, (at_x(g) * 4 + y) * 4 + r]
                    else:
                        w = tabrs[1, src, 2, (x * 4 + at_y(g)) * 4 + r]
                    piece = qv[h, g, src, r]
                    for i in range(8):
                        total[i] = total[i] + jnp.where(w == i, 1.0, 0.0).astype(F32) * piece
            for i in range(8):
                if g:
                    dv[h, g, i] = total[i]
                else:
                    ev[h, 0, i] = total[i]
            if g:
                device = ydev(g) if h else xdev(g)
                last.append(send(dv.at[h, g], ev.at[h, g], device, se.at[h, g], re.at[h, g]))

        if g == 1:
            for cp in gc:
                cp.wait_recv()
            held = gcr[0]
            for q in range(1, 8):
                held = held + gcr[q]
            ger[x, y] = held
            ge = [
                send(ger.at[x, y], ger.at[x, y], xydev(i, j), sge.at[i, j], rge.at[i, j])
                for i, j in PLANE
            ]

    for cp in oz:
        cp.wait_recv()
    for b in range(8):
        out[:, 128 * b : 128 * b + 128] = orv[b]
    for cp in last:
        cp.wait_recv()
    for h in range(2):
        for w in range(8):
            gf[16 * h : 16 * h + 16, 128 * w : 128 * w + 128] = (ev[h, 0, w] + ev[h, 1, w]) + (
                ev[h, 2, w] + ev[h, 3, w]
            )
    for cp in ge:
        cp.wait_recv()
    for a in range(4):
        for g in range(4):
            gwt[8 * a : 8 * a + 8, 128 * g : 128 * g + 128] = ger[a, g]
    for cp in pending:
        cp.wait_send()


def hand_over(a, b, c, out, gf, gwt, va, vb, vc, sem):
    trips = ((a, va, out), (b, vb, gf), (c, vc, gwt))
    inward = [pltpu.make_async_copy(src, via, sem.at[0, i]) for i, (src, via, _) in enumerate(trips)]
    outward = [pltpu.make_async_copy(via, dst, sem.at[1, i]) for i, (_, via, dst) in enumerate(trips)]
    for cp in inward:
        cp.start()
    for first, second in zip(inward, outward):
        first.wait()
        second.start()
    for cp in outward:
        cp.wait()


def on_device(feats_t, weight, cot_t, tiles, col_ids, counts):
    vmem = pl.BlockSpec(memory_space=pltpu.VMEM)
    hbm = pl.BlockSpec(memory_space=pltpu.HBM)

    def v(*shape):
        return pltpu.VMEM(shape, F32)

    def dma(*shape):
        return pltpu.SemaphoreType.DMA(shape)

    scratch = [
        v(8, 8, 128, 128),
        pltpu.VMEM((8, 4, 256, 256), BF16),
        v(8, 32, 128),
        v(8, 16, 128), v(8, 16, 128), v(8, 16, 128),
        v(8, 16, 128), v(8, 16, 128), v(8, 16, 128),
        v(2, 4, 4, 4, 16, 128),
        v(4, 4, 4, 32, 128),
        v(8, 32, 128),
        v(8, 2, 32, 128),
        v(8, 32, 512),
        pltpu.VMEM((512, 512), BF16),
        pltpu.VMEM((1024, 256), BF16),
        v(8, 32, 128),
        v(8, 32, 128),
        v(8, 32, 128),
        v(8, 2, 32, 128),
        v(8, 32, 128),
        v(8, 32, 128),
        v(8, 32, 128),
        v(4, 4, 8, 8, 128),
        v(4, 4, 8, 8, 128),
        v(8, 8, 128),
        v(8, 8, 128),
        v(4, 4, 8, 128),
        v(64, 32, 128),
        v(2, 4, 4, 4, 16, 128),
        v(2, 4, 4, 4, 16, 128),
        v(2, 4, 8, 16, 128),
        v(2, 4, 8, 16, 128),
        pltpu.VMEM((8, 128), I32),
        pltpu.VMEM((2, 4, 8, 128), I32),
        pltpu.SMEM((8, 128), I32),
        pltpu.SMEM((2, 4, 8, 128), I32),
        pltpu.SMEM((8, 8), I32),
        pltpu.SMEM((8,), I32),
        dma(8), dma(2), dma(12),
        dma(2, 4), dma(2, 4), dma(2, 4), dma(2, 4), dma(2, 4, 4), dma(2, 4, 4),
        dma(8), dma(8), dma(8), dma(8), dma(8), dma(8), dma(8), dma(8),
        pltpu.SemaphoreType.DMA, pltpu.SemaphoreType.DMA,
        dma(8), dma(8), dma(8), dma(8), dma(8), dma(8),
        dma(2, 4, 4), dma(2, 4, 4), dma(2, 4), dma(2, 4),
        dma(4, 4), dma(4, 4), dma(4, 4), dma(4, 4),
    ]
    out, gf, gwt = pl.pallas_call(
        kernel,
        out_shape=(
            jax.ShapeDtypeStruct((32, 1024), F32),
            jax.ShapeDtypeStruct((32, 1024), F32),
            jax.ShapeDtypeStruct((32, 512), F32),
        ),
        in_specs=[hbm] * 6,
        out_specs=(vmem, vmem, vmem),
        scratch_shapes=scratch,
        name="graph_layer",
        cost_estimate=pl.CostEstimate(flops=10**9, bytes_accessed=6 * 10**6, transcendentals=32768),
        compiler_params=pltpu.CompilerParams(
            collective_id=0, has_side_effects=True, vmem_limit_bytes=61936 * 1024
        ),
    )(feats_t, weight.T, cot_t, tiles, col_ids, counts)
    anywhere = pl.BlockSpec(memory_space=pl.ANY)
    out, gf, gwt = pl.pallas_call(
        hand_over,
        out_shape=(
            jax.ShapeDtypeStruct((32, 1024), F32),
            jax.ShapeDtypeStruct((32, 1024), F32),
            jax.ShapeDtypeStruct((32, 512), F32),
        ),
        in_specs=[anywhere] * 3,
        out_specs=(anywhere,) * 3,
        scratch_shapes=[v(32, 1024), v(32, 1024), v(32, 512), dma(2, 3)],
        name="hand_over",
        cost_estimate=pl.CostEstimate(flops=0, bytes_accessed=2 * 320 * 1024, transcendentals=0),
    )(out, gf, gwt)
    return out, gf, gwt.T


def solution(mesh):
    return jax.shard_map(
        on_device,
        mesh=mesh,
        in_specs=(
            P("feat", "node"),
            P(None, "feat"),
            P("feat", "node"),
            P("node", None, None, None),
            P("node", None),
            P("node"),
        ),
        out_specs=(P("feat", "node"), P("feat", "node"), P(None, "feat")),
        check_vma=False,
    )
```

```python
import jax
import jax.numpy as jnp
from jax import lax
from jax.experimental import pallas as pl
from jax.experimental.pallas import tpu as pltpu
from jax.sharding import PartitionSpec as P

MESH = pl.DeviceIdType.MESH
F32 = jnp.float32
BF16 = jnp.bfloat16
I32 = jnp.int32
NN = (((1,), (0,)), ((), ()))
NT = (((1,), (1,)), ((), ()))
FAR = (4, 3, 5, 2, 6, 1, 7)
PLANE = sorted(((i, j) for i in range(4) for j in range(4) if i + j), key=lambda d: -min(d[0], 4 - d[0]) - min(d[1], 4 - d[1]))


def split(v):
    hi = v.astype(BF16)
    return hi, (v - hi.astype(F32)).astype(BF16)


def mm(a, b, dims):
    return lax.dot_general(a, b, dims, preferred_element_type=F32)


def kernel(
    feats, wt, cot, tiles, cols_h, counts_h,
    out, gf, gwt,
    t32, tb, fo, a01, a02, a03, a11, a12, a13, sv, rv, mx, mv, wa, wst, wn, ca,
    oo, orv, pv, px, gs, gv, wp, gar, gcs, gcr, ger,
    cv, sb, qv, dv, ev, tab, tabr, tabs, tabrs, cols, counts,
    sem_t, sem_s, sem_i,
    s1, r1, s1t, r1t, s2, r2, sw, rw, sc, rc, sm, rm, sf, rf, sp, rp,
    so, ro, sg, rg, sgw, rgw, sq, rq, se, re, sga, rga, sge, rge,
):
    node = lax.axis_index("node")
    feat = lax.axis_index("feat")
    x, y = lax.div(node, 4), lax.rem(node, 4)
    z, c = lax.div(feat, 2), lax.rem(feat, 2)
    oc = 1 - c

    def at_x(d):
        return lax.rem(x + d, 4)

    def at_y(d):
        return lax.rem(y + d, 4)

    def at_z(d):
        return lax.rem(z + d, 8)

    def xdev(d):
        return (at_x(d) * 4 + y, feat)

    def ydev(d):
        return (x * 4 + at_y(d), feat)

    def xydev(dx, dy):
        return (at_x(dx) * 4 + at_y(dy), feat)

    def zdev(d):
        return (node, at_z(d) * 2 + c)

    cdev = (node, z * 2 + oc)
    pending = []

    def send(src, dst, device, ss, rs):
        cp = pltpu.make_async_remote_copy(
            src_ref=src, dst_ref=dst, send_sem=ss, recv_sem=rs,
            device_id=device, device_id_type=MESH,
        )
        cp.start()
        pending.append(cp)
        return cp

    ids = [
        pltpu.make_async_copy(cols_h, cols, sem_i.at[0]),
        pltpu.make_async_copy(counts_h, counts, sem_i.at[1]),
    ]
    fcopies = [
        pltpu.make_async_copy(feats.at[:, pl.ds(128 * w, 128)], fo.at[w], sem_i.at[2 + w])
        for w in range(8)
    ]
    own = [
        pltpu.make_async_copy(wt, wa.at[z], sem_i.at[10]),
        pltpu.make_async_copy(cot.at[:, pl.ds(pl.multiple_of(z * 128, 128), 128)], ca.at[z], sem_i.at[11]),
    ]
    for cp in fcopies + ids + own:
        cp.start()
    for b in range(8):
        pltpu.make_async_copy(tiles.at[b], t32.at[b], sem_t.at[b]).start()
    barrier = pltpu.get_barrier_semaphore()
    peers = [zdev(d) for d in (4, 3, 5, 2, 6, 1, 7)] + [xydev(*d) for d in PLANE] + [cdev]
    for p in peers:
        pl.semaphore_signal(barrier, 1, device_id=p, device_id_type=MESH)

    for cp in ids:
        cp.wait()
    lane8 = lax.broadcasted_iota(I32, (8, 128), 1)
    sub8 = lax.broadcasted_iota(I32, (8, 128), 0)
    by_lane = jnp.full((8, 128), 1024, I32)
    for s in range(64):
        by_lane = jnp.where(lane8 == s, cols[s // 8, s % 8], by_lane)
    place_l = jnp.zeros((8, 128), I32)
    rows = []
    for g in range(8):
        by_sub = jnp.zeros((8, 128), I32)
        for k in range(8):
            by_sub = jnp.where(sub8 == k, cols[g, k], by_sub)
        rows.append(by_sub)
    own_l = lax.shift_right_logical(by_lane, 3)
    slot_sum = jnp.zeros((8, 128), I32)
    want_sum = jnp.zeros((8, 128), I32)
    for g in range(8):
        own_s = lax.shift_right_logical(rows[g], 3)
        slot_s = sub8 + 8 * g
        same = own_s == own_l
        place_l = place_l + jnp.where(same & (slot_s < lane8), 1, 0)
        rank = jnp.sum(jnp.where(same & (lane8 < slot_s), 1, 0), axis=1, keepdims=True)
        hit = (own_s * 4 + rank) == lane8
        slot_sum = slot_sum + jnp.where(hit, slot_s, 0)
        want_sum = want_sum + jnp.where(hit, rows[g] & 7, 0)
    place = own_l * 4 + jnp.sum(place_l, axis=0, keepdims=True)
    slot_of = jnp.sum(slot_sum, axis=0, keepdims=True)
    want = jnp.sum(want_sum, axis=0, keepdims=True)
    table = jnp.where(sub8 == 0, place, jnp.where(sub8 == 1, slot_of, want))
    tab[...] = table
    tabr[0, y] = table
    tabr[1, x] = table
    for cp in fcopies:
        cp.wait()
    pl.semaphore_wait(barrier, len(peers))

    heard = ((None, a01, a02, a03), (None, a11, a12, a13))
    fx, fy = {}, {}
    for d in (1, 3, 2):
        fx[d] = send(fo.at[:, pl.ds(0, 16)], heard[0][d], xdev(d), s1.at[0, d], r1.at[0, d])
        fy[d] = send(fo.at[:, pl.ds(16, 16)], heard[1][d], ydev(d), s1.at[1, d], r1.at[1, d])

    tx = [send(tab, tabr.at[1, x], xdev(d), s1t.at[0, d], r1t.at[0, d]) for d in (1, 2, 3)]
    ty = [send(tab, tabr.at[0, y], ydev(d), s1t.at[1, d], r1t.at[1, d]) for d in (1, 2, 3)]
    to_s = pltpu.make_async_copy(tab, tabs, sem_s.at[0])
    to_s.start()
    cz = [send(cot.at[:, pl.ds(pl.multiple_of(at_z(d) * 128, 128), 128)], ca.at[z], zdev(d), sc.at[d], rc.at[d]) for d in FAR]
    wz = [send(wt, wa.at[z], zdev(d), sw.at[d], rw.at[d]) for d in FAR]
    to_s.wait()
    for cp in tx + ty:
        cp.wait_recv()
    to_rs = pltpu.make_async_copy(tabr, tabrs, sem_s.at[1])
    to_rs.start()
    to_rs.wait()

    leg2 = []
    for g in (0, 1, 3, 2):
        for h in range(2):
            if g:
                (fx, fy)[h][g].wait_recv()
            xo, yo = at_x(4 - g), at_y(4 - g)
            for d in (2, 1, 3, 0):
                for r in range(4):
                    if h == 0:
                        w = tabrs[0, at_y(d), 2, (xo * 4 + y) * 4 + r]
                    else:
                        w = tabrs[1, at_x(d), 2, (x * 4 + yo) * 4 + r]
                    block = heard[h][g][w] if g else fo[w, 16 * h : 16 * h + 16]
                    if d:
                        sv[h, g, d, r] = block
                    elif h == 0:
                        rv[xo, y, r, 0:16] = block
                    else:
                        rv[x, yo, r, 16:32] = block
                if d and h == 0:
                    to = rv.at[xo, y, :, pl.ds(0, 16)]
                    leg2.append(send(sv.at[0, g, d], to, ydev(d), s2.at[0, g, d], r2.at[0, g, d]))
                elif d:
                    to = rv.at[x, yo, :, pl.ds(16, 16)]
                    leg2.append(send(sv.at[1, g, d], to, xdev(d), s2.at[1, g, d], r2.at[1, g, d]))

    def convert(b, carry):
        pltpu.make_async_copy(tiles.at[b], t32.at[b], sem_t.at[b]).wait()
        for k in range(8):
            live = jnp.where(k < counts[b], 1.0, 0.0).astype(F32)
            hi, lo = split(t32[b, k] * live)
            q = 128 * (k % 2)
            tb[b, k // 2, 0:128, q : q + 128] = hi
            tb[b, k // 2, 128:256, q : q + 128] = lo
        return carry

    lax.fori_loop(0, 8, convert, 0)

    for cp in leg2:
        cp.wait_recv()

    mz = []
    for d in FAR + (0,):
        b = at_z(d)
        acc = None
        for kp in range(4):
            parts = []
            for k in (2 * kp, 2 * kp + 1):
                p = tabs[0, b * 8 + k]
                parts.append(
                    split(rv[lax.shift_right_logical(p, 4), lax.shift_right_logical(p, 2) & 3, p & 3])
                )
            lhs = jnp.concatenate(
                [
                    jnp.concatenate([parts[0][0], parts[1][0]], axis=1),
                    jnp.concatenate([parts[0][1], parts[1][1]], axis=1),
                ],
                axis=0,
            )
            term = mm(lhs, tb[b, kp], NT)
            acc = term if acc is None else acc + term
        mixed = (acc[32:64, 128:256] + acc[32:64, 0:128] + acc[0:32, 128:256]) + acc[0:32, 0:128]
        if d:
            mx[d] = mixed
            mz.append(send(mx.at[d], mv.at[z, c], zdev(d), sm.at[d], rm.at[d]))
        else:
            mv[z, c] = mixed
    for cp in wz:
        cp.wait_recv()
    for cp in own:
        cp.wait()
    for q in range(8):
        hi, lo = split(wa[q])
        wst[32 * q : 32 * q + 32] = hi
        wst[256 + 32 * q : 288 + 32 * q] = lo
    for g in range(4):
        turned = jnp.transpose(wa[:, :, 128 * g : 128 * g + 128].reshape(256, 128))
        hi, lo = split(turned)
        wn[128 * g : 128 * g + 128] = hi
        wn[512 + 128 * g : 640 + 128 * g] = lo

    fz = [send(mv.at[z, c], mv.at[z, c], cdev, sf.at[0], rf.at[0])]
    for d in (2, 6, 1, 7, 3, 5, 4):
        mz[FAR.index(d)].wait_recv()
        q = at_z(8 - d)
        fz.append(send(mv.at[q, c], mv.at[q, c], cdev, sf.at[d], rf.at[d]))
    for cp in cz:
        cp.wait_recv()
    for cp in fz:
        cp.wait_recv()

    hi, lo = split(mv[...].reshape(512, 128))
    mhl = jnp.concatenate([hi, lo], axis=1)
    r = mm(wst[...], mhl, NN)
    pre = (r[256:512, 128:256] + r[256:512, 0:128] + r[0:256, 128:256]) + r[0:256, 0:128]
    sig = jax.nn.sigmoid(pre)
    gp = ca[...].reshape(256, 128) * (sig * (1.0 + pre * (1.0 - sig)))
    ghi, glo = split(gp)
    r = mm(wn[...], jnp.concatenate([ghi, glo], axis=1), NN)
    part = (r[512:1024, 128:256] + r[512:1024, 0:128] + r[0:512, 128:256]) + r[0:512, 0:128]
    pv[...] = part.reshape(8, 2, 32, 128)
    xc = send(pv.at[:, oc], px, cdev, sp, rp)
    oo[...] = (pre * sig).reshape(8, 32, 128)
    g2 = jnp.concatenate(
        [jnp.concatenate([ghi, ghi], axis=1), jnp.concatenate([glo, glo], axis=1)], axis=0
    )
    r = mm(g2, mhl, NT)
    r = r[0:256] + r[256:512]
    for q in range(8):
        for a in range(4):
            for g in range(4):
                chunk = r[32 * q + 8 * a : 32 * q + 8 * a + 8, 128 * g : 128 * g + 128]
                wp[a, g, q] = chunk
    xc.wait_recv()
    gz = []
    for d in FAR:
        gs[at_z(d)] = pv[at_z(d), c] + px[at_z(d)]
        gz.append(send(gs.at[at_z(d)], gv.at[z], zdev(d), sg.at[d], rg.at[d]))
    gv[z] = pv[z, c] + px[z]
    ga = [
        send(wp.at[at_x(i), at_y(j)], gar.at[x, y], xydev(i, j), sga.at[i, j], rga.at[i, j])
        for i, j in PLANE
    ]
    gar[x, y] = wp[x, y]
    orv[z] = oo[z]

    arrivals = {d: cp for d, cp in zip(FAR, gz)}
    for d in (0, 1, 7, 2, 6, 3, 5, 4):
        if d:
            arrivals[d].wait_recv()
        b = at_z(8 - d)
        ghi, glo = split(gv[b])
        lhs = jnp.concatenate(
            [jnp.concatenate([ghi, ghi], axis=1), jnp.concatenate([glo, glo], axis=1)], axis=0
        )
        for kp in range(4):
            r = mm(lhs, tb[b, kp], NN)
            r = r[0:32] + r[32:64]
            cv[b * 8 + 2 * kp] = r[:, 0:128]
            cv[b * 8 + 2 * kp + 1] = r[:, 128:256]

    back = {}
    for g in (2, 1, 3, 0):
        for h in range(2):
            for d in (2, 1, 3, 0):
                for r in range(4):
                    if h == 0:
                        s = tabs[1, (at_x(g) * 4 + at_y(d)) * 4 + r]
                    else:
                        s = tabs[1, (at_x(d) * 4 + at_y(g)) * 4 + r]
                    piece = cv[s, 16 * h : 16 * h + 16]
                    if d:
                        sb[h, g, d, r] = piece
                    elif h == 0:
                        qv[0, g, y, r] = piece
                    else:
                        qv[1, g, x, r] = piece
                if d and h == 0:
                    to = qv.at[0, g, y]
                    back[h, g, d] = send(sb.at[0, g, d], to, ydev(d), sq.at[0, g, d], rq.at[0, g, d])
                elif d:
                    to = qv.at[1, g, x]
                    back[h, g, d] = send(sb.at[1, g, d], to, xdev(d), sq.at[1, g, d], rq.at[1, g, d])

    oz = [send(oo.at[at_z(d)], orv.at[z], zdev(d), so.at[d], ro.at[d]) for d in FAR]

    for cp in ga:
        cp.wait_recv()
    held = gar[0, 0]
    for q in range(1, 16):
        held = held + gar[q // 4, q % 4]
    gcs[...] = held
    gc = [send(gcs.at[at_z(d)], gcr.at[z], zdev(d), sgw.at[d], rgw.at[d]) for d in FAR]
    gcr[z] = gcs[z]

    last = []
    for g in (2, 1, 3, 0):
        for h in range(2):
            for d in (1, 3, 2):
                back[h, g, d].wait_recv()
            for part in range(2):
                total = [jnp.zeros((16, 128), F32) for _ in range(4)]
                for src in range(4):
                    for r in range(4):
                        if h == 0:
                            w = tabrs[0, src, 2, (at_x(g) * 4 + y) * 4 + r]
                        else:
                            w = tabrs[1, src, 2, (x * 4 + at_y(g)) * 4 + r]
                        piece = qv[h, g, src, r]
                        for i in range(4):
                            named = jnp.where(w == 4 * part + i, 1.0, 0.0).astype(F32)
                            total[i] = total[i] + named * piece
                for i in range(4):
                    if g:
                        dv[h, g, 4 * part + i] = total[i]
                    else:
                        ev[h, 0, 4 * part + i] = total[i]
                if g:
                    device = ydev(g) if h else xdev(g)
                    piece = pl.ds(4 * part, 4)
                    last.append(
                        send(dv.at[h, g, piece], ev.at[h, g, piece], device, se.at[h, g, part], re.at[h, g, part])
                    )

        if g == 1:
            for cp in gc:
                cp.wait_recv()
            held = gcr[0]
            for q in range(1, 8):
                held = held + gcr[q]
            ger[x, y] = held
            ge = [
                send(ger.at[x, y], ger.at[x, y], xydev(i, j), sge.at[i, j], rge.at[i, j])
                for i, j in PLANE
            ]

    for cp in oz:
        cp.wait_recv()
    for b in range(8):
        out[:, 128 * b : 128 * b + 128] = orv[b]
    for cp in last:
        cp.wait_recv()
    for h in range(2):
        for w in range(8):
            gf[16 * h : 16 * h + 16, 128 * w : 128 * w + 128] = (ev[h, 0, w] + ev[h, 1, w]) + (
                ev[h, 2, w] + ev[h, 3, w]
            )
    for cp in ge:
        cp.wait_recv()
    for a in range(4):
        for g in range(4):
            gwt[8 * a : 8 * a + 8, 128 * g : 128 * g + 128] = ger[a, g]
    for cp in pending:
        cp.wait_send()


def hand_over(a, b, c, out, gf, gwt, va, vb, vc, sem):
    trips = ((a, va, out), (b, vb, gf), (c, vc, gwt))
    inward = [pltpu.make_async_copy(src, via, sem.at[0, i]) for i, (src, via, _) in enumerate(trips)]
    outward = [pltpu.make_async_copy(via, dst, sem.at[1, i]) for i, (_, via, dst) in enumerate(trips)]
    for cp in inward:
        cp.start()
    for first, second in zip(inward, outward):
        first.wait()
        second.start()
    for cp in outward:
        cp.wait()


def on_device(feats_t, weight, cot_t, tiles, col_ids, counts):
    vmem = pl.BlockSpec(memory_space=pltpu.VMEM)
    hbm = pl.BlockSpec(memory_space=pltpu.HBM)

    def v(*shape):
        return pltpu.VMEM(shape, F32)

    def dma(*shape):
        return pltpu.SemaphoreType.DMA(shape)

    scratch = [
        v(8, 8, 128, 128),
        pltpu.VMEM((8, 4, 256, 256), BF16),
        v(8, 32, 128),
        v(8, 16, 128), v(8, 16, 128), v(8, 16, 128),
        v(8, 16, 128), v(8, 16, 128), v(8, 16, 128),
        v(2, 4, 4, 4, 16, 128),
        v(4, 4, 4, 32, 128),
        v(8, 32, 128),
        v(8, 2, 32, 128),
        v(8, 32, 512),
        pltpu.VMEM((512, 512), BF16),
        pltpu.VMEM((1024, 256), BF16),
        v(8, 32, 128),
        v(8, 32, 128),
        v(8, 32, 128),
        v(8, 2, 32, 128),
        v(8, 32, 128),
        v(8, 32, 128),
        v(8, 32, 128),
        v(4, 4, 8, 8, 128),
        v(4, 4, 8, 8, 128),
        v(8, 8, 128),
        v(8, 8, 128),
        v(4, 4, 8, 128),
        v(64, 32, 128),
        v(2, 4, 4, 4, 16, 128),
        v(2, 4, 4, 4, 16, 128),
        v(2, 4, 8, 16, 128),
        v(2, 4, 8, 16, 128),
        pltpu.VMEM((8, 128), I32),
        pltpu.VMEM((2, 4, 8, 128), I32),
        pltpu.SMEM((8, 128), I32),
        pltpu.SMEM((2, 4, 8, 128), I32),
        pltpu.SMEM((8, 8), I32),
        pltpu.SMEM((8,), I32),
        dma(8), dma(2), dma(12),
        dma(2, 4), dma(2, 4), dma(2, 4), dma(2, 4), dma(2, 4, 4), dma(2, 4, 4),
        dma(8), dma(8), dma(8), dma(8), dma(8), dma(8), dma(8), dma(8),
        pltpu.SemaphoreType.DMA, pltpu.SemaphoreType.DMA,
        dma(8), dma(8), dma(8), dma(8), dma(8), dma(8),
        dma(2, 4, 4), dma(2, 4, 4), dma(2, 4, 2), dma(2, 4, 2),
        dma(4, 4), dma(4, 4), dma(4, 4), dma(4, 4),
    ]
    out, gf, gwt = pl.pallas_call(
        kernel,
        out_shape=(
            jax.ShapeDtypeStruct((32, 1024), F32),
            jax.ShapeDtypeStruct((32, 1024), F32),
            jax.ShapeDtypeStruct((32, 512), F32),
        ),
        in_specs=[hbm] * 6,
        out_specs=(vmem, vmem, vmem),
        scratch_shapes=scratch,
        name="graph_layer",
        cost_estimate=pl.CostEstimate(flops=10**9, bytes_accessed=6 * 10**6, transcendentals=32768),
        compiler_params=pltpu.CompilerParams(
            collective_id=0, has_side_effects=True, vmem_limit_bytes=61936 * 1024
        ),
    )(feats_t, weight.T, cot_t, tiles, col_ids, counts)
    anywhere = pl.BlockSpec(memory_space=pl.ANY)
    out, gf, gwt = pl.pallas_call(
        hand_over,
        out_shape=(
            jax.ShapeDtypeStruct((32, 1024), F32),
            jax.ShapeDtypeStruct((32, 1024), F32),
            jax.ShapeDtypeStruct((32, 512), F32),
        ),
        in_specs=[anywhere] * 3,
        out_specs=(anywhere,) * 3,
        scratch_shapes=[v(32, 1024), v(32, 1024), v(32, 512), dma(2, 3)],
        name="hand_over",
        cost_estimate=pl.CostEstimate(flops=0, bytes_accessed=2 * 320 * 1024, transcendentals=0),
    )(out, gf, gwt)
    return out, gf, gwt.T


def solution(mesh):
    return jax.shard_map(
        on_device,
        mesh=mesh,
        in_specs=(
            P("feat", "node"),
            P(None, "feat"),
            P("feat", "node"),
            P("node", None, None, None),
            P("node", None),
            P("node"),
        ),
        out_specs=(P("feat", "node"), P("feat", "node"), P(None, "feat")),
        check_vma=False,
    )
```
